32 devices in a mesh: node: 1, group: 32 (over z, y, x, core), fsdp: 1.
Axes of the slice: x: 2, y: 2, z: 4, core: 2. Of those that a mesh axis runs over, the one named last changes fastest.
Arguments:
- grad_values: bfloat16 [1, 32, 1, 128, 12288], P('node', 'group', 'fsdp'), may hold values from -6 to 6
- grad_scales: bfloat16 [1, 32, 1, 128, 96], P('node', 'group', 'fsdp'), may hold values from 0.5 to 4
- master: float32 [1, 128, 12288], P('fsdp', 'group'), may hold values from -6 to 6
- first_moment: bfloat16 [1, 128, 12288], P('fsdp', 'group'), may hold values from -1 to 1
- first_scale: float32 [1, 128, 96], P('fsdp', 'group'), may hold values from 0.5 to 2
- second_moment: bfloat16 [1, 128, 12288], P('fsdp', 'group'), may hold values from 0.049804688 to 1
- second_scale: float32 [1, 128, 96], P('fsdp', 'group'), may hold values from 10 to 100
Outputs:
- new_master: float32 [1, 128, 12288], P('fsdp', 'group')
- new_first: bfloat16 [1, 128, 12288], P('fsdp', 'group')
- new_first_scale: float32 [1, 128, 96], P('fsdp', 'group')
- new_second: bfloat16 [1, 128, 12288], P('fsdp', 'group')
- new_second_scale: float32 [1, 128, 96], P('fsdp', 'group')
- weights: bfloat16 [1, 128, 12288], P('fsdp')
- transposed: bfloat16 [1, 12288, 128], P('fsdp')
The draws below stay inside these ranges and needn't reach their ends.
All inputs are finite; a program needn't handle non-finite values. Where the reference program divides by a largest or mean magnitude, that divisor is 1e-20 or more.
Results may differ from the reference program's by a relative error of at most 0.001.
Values may be sent and summed in bfloat16 or wider, within the bound.
A program may use at most 128 MiB of HBM per device.

```python
import math
import jax
import jax.numpy as jnp
from jax import lax

D = 12288
BLOCK = 128
ROWS_SHARD = 128
N_NODE = 1
N_GROUP = 32
N_FSDP = 1


def strengthened(values, key, source, target, shards_of, factor):
    owner, partner = [(jnp.arange(values.shape[position]) // (values.shape[position] // shards_of)).reshape([-1 if axis == position else 1 for axis in range(values.ndim)]) for position in (source, target)]
    chosen = jax.random.permutation(key, shards_of)[partner]
    strong = (owner == chosen) | (owner == (partner + shards_of // 2) % shards_of)
    return jnp.where(strong, factor * values, values)


def level_of(own_key, dims, cuts, least, largest):
    def one(position, parts):
        heights = jax.random.uniform(jax.random.fold_in(jax.random.fold_in(own_key, 6), position), (parts,), jnp.float32, least / len(cuts), largest / len(cuts))
        return jnp.repeat(jnp.exp(heights), dims[position] // parts).reshape((-1,) + (1,) * (len(dims) - position - 1))

    factor_of = one(*cuts[0])
    for cut in cuts[1:]:
        factor_of = factor_of * one(*cut)
    return factor_of


def bell_draw(own_key, shape, deviation, bound, cuts=(), held_as=jnp.bfloat16):
    factor_of = level_of(own_key, shape, cuts, -0.22, 0.18) if cuts else 1.0
    drawn = jax.random.normal(own_key, shape, jnp.float32) * deviation * factor_of
    return jnp.minimum(jnp.maximum(drawn, -bound), bound).astype(held_as)


def noise_with(stream_key, extent, deviation, limit, split, heavy, dtype=jnp.bfloat16):
    values = deviation * jax.random.normal(stream_key, extent, jnp.float32)
    if split:
        values = values * level_of(stream_key, extent, split, -0.22, 0.18)
    return jnp.clip(strengthened(values, jax.random.fold_in(stream_key, 3), *heavy), -limit, limit).astype(dtype)


def setup_inputs(seed: int = 0) -> dict:
    streams_of = jax.random.split(jax.random.key(seed), 8)
    return {
        "grad_values": noise_with(streams_of[0], (N_NODE, N_GROUP, N_FSDP, ROWS_SHARD, D), 1.0, 6.0, ((1, 32),), (1, 3, 32, 2.75)),
        "grad_scales": jnp.clip(jnp.exp(math.log(4.0) - 2.0794415 * jax.random.uniform(streams_of[1], (N_NODE, N_GROUP, N_FSDP, ROWS_SHARD, D // BLOCK), jnp.float32) ** level_of(streams_of[1], (N_NODE, N_GROUP, N_FSDP, ROWS_SHARD, D // BLOCK), ((1, 32),), -0.2, 0.2)), 0.5, 4.0).astype(jnp.bfloat16),
        "master": bell_draw(streams_of[2], (N_FSDP, ROWS_SHARD, D), 1.0, 6.0, ((1, 32),), jnp.float32),
        "first_moment": jnp.clip(jax.random.uniform(streams_of[3], (N_FSDP, ROWS_SHARD, D), jnp.float32, -1.0, 1.0) * level_of(streams_of[3], (N_FSDP, ROWS_SHARD, D), ((1, 32),), -0.4, 0.0), -1.0, 1.0).astype(jnp.bfloat16),
        "first_scale": jnp.clip(jnp.exp(math.log(2.0) - 1.3862944 * jax.random.uniform(streams_of[4], (N_FSDP, ROWS_SHARD, D // BLOCK), jnp.float32) ** level_of(streams_of[4], (N_FSDP, ROWS_SHARD, D // BLOCK), ((1, 32),), -0.2, 0.2)), 0.5, 2.0),
        "second_moment": jnp.clip(0.049804688 + 0.9501953 * jax.random.uniform(streams_of[5], (N_FSDP, ROWS_SHARD, D), jnp.float32) ** level_of(streams_of[5], (N_FSDP, ROWS_SHARD, D), ((1, 32),), -0.2, 0.2), 0.049804688, 1.0).astype(jnp.bfloat16),
        "second_scale": jnp.clip(jnp.exp(math.log(100.0) - 2.3025851 * jax.random.uniform(streams_of[6], (N_FSDP, ROWS_SHARD, D // BLOCK), jnp.float32) ** level_of(streams_of[6], (N_FSDP, ROWS_SHARD, D // BLOCK), ((1, 32),), -0.2, 0.2)), 10.0, 100.0),
    }


beta_one = 0.9
beta_two = 0.95
rate = 0.02
adam_eps = 1e-08
scale_eps = 1e-06
corr_one = 1.0 - 0.9 ** 10
corr_two = 1.0 - 0.95 ** 10

def expand(values, scales):
    shape = values.shape
    blocks = values.astype(jnp.float32).reshape(shape[:-1] + (shape[-1] // BLOCK, BLOCK))
    return (blocks * scales.astype(jnp.float32)[..., None]).reshape(shape)

def quantize(values, signed):
    shape = values.shape
    blocks = values.reshape(shape[:-1] + (shape[-1] // BLOCK, BLOCK))
    if signed:
        peak = lax.optimization_barrier(jnp.max(jnp.abs(blocks), axis=-1)) + scale_eps
    else:
        peak = lax.optimization_barrier(jnp.max(blocks, axis=-1)) + scale_eps
    coded = (blocks / peak[..., None]).astype(jnp.bfloat16).reshape(shape)
    return (coded, peak)

def adam_step(gradient, master, first_moment, first_scale, second_moment, second_scale):
    first = beta_one * expand(first_moment, first_scale) + (1.0 - beta_one) * gradient
    second = beta_two * expand(second_moment, second_scale) + (1.0 - beta_two) * gradient * gradient
    direction = first / corr_one / (jnp.sqrt(second / corr_two) + adam_eps)
    updated = master - rate * direction
    first_coded, first_peak = quantize(first, True)
    second_coded, second_peak = quantize(second, False)
    return (updated, first_coded, first_peak, second_coded, second_peak, updated.astype(jnp.bfloat16))

def reference(grad_values, grad_scales, master, first_moment, first_scale, second_moment, second_scale):
    count = grad_values.shape[0] * grad_values.shape[1]
    flat_values = grad_values.reshape((count,) + grad_values.shape[2:])
    flat_scales = grad_scales.reshape((count,) + grad_scales.shape[2:])

    def accumulate(total, pair):
        return (total + expand(pair[0], pair[1]), None)
    start = jnp.zeros(grad_values.shape[2:], jnp.float32)
    gradient, unused = lax.scan(accumulate, start, (flat_values, flat_scales))
    result = adam_step(gradient, master, first_moment, first_scale, second_moment, second_scale)
    updated, first_coded, first_peak, second_coded, second_peak, weights = result
    transposed = jnp.swapaxes(weights, 1, 2)
    return (updated, first_coded, first_peak, second_coded, second_peak, weights, transposed)
```

```python
import functools

import jax
import jax.numpy as jnp
from jax import lax
from jax.experimental import pallas as pl
from jax.experimental.pallas import tpu as pltpu
from jax.sharding import PartitionSpec as P

BLOCK = 128
CHUNKS = 4
GROUPS = 2
TILE = 16

beta_one = 0.9
beta_two = 0.95
rate = 0.02
adam_eps = 1e-08
scale_eps = 1e-06
corr_one = 1.0 - 0.9**10
corr_two = 1.0 - 0.95**10

f32 = jnp.float32
bf16 = jnp.bfloat16


def exchange_kernel(
    grad, gscale, master, fm, fs, sm, ss,
    comm, new_master, new_first, new_fs, new_second, new_ss,
    own, sib, sc_sib, sh_own, sh_sib, part, rx1, rx2, acc, rx3, gfull, fbase, sbase, slotf, slot,
    own_sem, sc_sem, sib_sem, p1_sem, p2_sem, z_sem, g_sem,
    az_sem, ax_sem, ay_sem, fx_sem, fy_sem, as_sem, loc_sem,
):
    half = grad.shape[1] // 2
    w = half // CHUNKS
    nb = w // BLOCK
    hb = half // BLOCK
    me = lax.axis_index("group")
    c = lax.rem(me, 2)
    x = lax.rem(me // 2, 2)
    y = lax.rem(me // 4, 2)
    z = me // 8

    def index(zz, yy, xx, cc):
        return zz * 8 + yy * 4 + xx * 2 + cc

    sibling = index(z, y, x, 1 - c)
    xn = index(z, y, 1 - x, c)
    yn = index(z, 1 - y, x, c)
    z_up = [lax.rem(z + d, 4) for d in range(4)]
    z_from = [lax.rem(z + 4 - d, 4) for d in range(4)]
    zn = [index(z_up[d], y, x, c) for d in range(4)]

    def remote(src, dst, sems, at, to):
        return pltpu.make_async_remote_copy(
            src_ref=src,
            dst_ref=dst,
            send_sem=sems.at[(0,) + at],
            recv_sem=sems.at[(1,) + at],
            device_id={"group": to},
            device_id_type=pl.DeviceIdType.MESH,
        )

    sent = []

    def send(*args):
        copy = remote(*args)
        copy.start()
        sent.append(copy)
        return copy

    barrier = pltpu.get_barrier_semaphore()
    partners = [sibling, xn, yn] + zn[1:]
    for to in partners:
        pl.semaphore_signal(
            barrier, inc=1, device_id={"group": to}, device_id_type=pl.DeviceIdType.MESH
        )
    pl.semaphore_wait(barrier, len(partners))

    scale_copy = send(gscale, sc_sib, sc_sem, (0,), sibling)
    sib_copies, own_copies = [], []
    for k in range(CHUNKS):
        there = pl.multiple_of((1 - c) * half + k * w, BLOCK)
        here = pl.multiple_of(c * half + k * w, BLOCK)
        sib_copies.append(send(grad.at[:, pl.ds(there, w)], sib.at[k], sib_sem, (k,), sibling))
        copy = pltpu.make_async_copy(grad.at[:, pl.ds(here, w)], own.at[k], own_sem.at[k])
        copy.start()
        own_copies.append(copy)

    def half_scales(ref):
        values = ref[...].astype(f32)
        return jnp.where(c == 0, values[:, :hb], values[:, hb:])

    sh_own[...] = half_scales(gscale)
    scale_copy.wait_recv()
    sh_sib[...] = half_scales(sc_sib)

    def order(k):
        return (x, y, xn, yn) if k % 2 == 0 else (y, x, yn, xn)

    p1, p2, gc = {}, {}, {}

    def core_sum(k):
        own_copies[k].wait()
        sib_copies[k].wait_recv()

        def body(i, carry):
            rows = pl.ds(pl.multiple_of(i * 16, 16), 16)
            so, sb = sh_own[rows, :], sh_sib[rows, :]
            zz, yy = i // 2, lax.rem(i, 2)
            for b in range(nb):
                j = k * nb + b
                cols = pl.ds(b * BLOCK, BLOCK)
                v = own[k, rows, cols].astype(f32) * so[:, j : j + 1]
                v += sib[k, rows, cols].astype(f32) * sb[:, j : j + 1]
                for xx in range(2):
                    one, two = (xx, yy) if k % 2 == 0 else (yy, xx)
                    part[k, one, two, zz, :, cols] = v[8 * xx : 8 * xx + 8]
            return carry

        lax.fori_loop(0, 8, body, 0)
        a, _, an, _ = order(k)
        p1[k] = send(part.at[k, 1 - a], rx1.at[k], p1_sem, (k,), an)

    def base(k):
        for h in range(2):
            for b in range(nb):
                j = h * hb + k * nb + b
                cols = pl.ds(j * BLOCK, BLOCK)
                fbase[:, cols] = beta_one * (fm[:, cols].astype(f32) * fs[:, j : j + 1])
                sbase[:, cols] = beta_two * (sm[:, cols].astype(f32) * ss[:, j : j + 1])

    def first_axis(k):
        a, b, _, bn = order(k)
        p1[k].wait_recv()
        for zz in range(4):
            part[k, a, 1 - b, zz] = part[k, a, 1 - b, zz] + rx1[k, 1 - b, zz]
        p2[k] = send(part.at[k, a, 1 - b], rx2.at[k], p2_sem, (k,), bn)

    def second_axis(k):
        a, b, _, _ = order(k)
        p2[k].wait_recv()
        for zz in range(4):
            acc[k, zz] = part[k, a, b, zz] + rx1[k, b, zz] + rx2[k, zz]
        for d in range(1, 4):
            send(acc.at[k, z_up[d]], rx3.at[k, d], z_sem, (k, d), zn[d])

    def along_z(k):
        total = acc[k, z]
        for d in range(1, 4):
            remote(acc.at[k, z_up[d]], rx3.at[k, d], z_sem, (k, d), zn[d]).wait_recv()
            total = total + rx3[k, d]
        gfull[c, k] = total
        gc[k] = send(gfull.at[c, k], gfull.at[c, k], g_sem, (k,), sibling)

    def adam(k):
        remote(gfull.at[1 - c, k], gfull.at[1 - c, k], g_sem, (k,), sibling).wait_recv()
        for h in range(2):
            cols = pl.ds(h * half + k * w, w)
            v = gfull[h, k]
            g = jnp.where(c == 0, v[0:4], v[4:8])
            first = fbase[:, cols] + (1.0 - beta_one) * g
            second = sbase[:, cols] + (1.0 - beta_two) * g * g
            fbase[:, cols] = first
            sbase[:, cols] = second
            direction = first / corr_one / (jnp.sqrt(second / corr_two) + adam_eps)
            updated = master[:, cols] - rate * direction
            new_master[:, cols] = updated
            for q in range(2):
                r = 4 * (2 * h + q)
                slotf[r : r + 4, k * (w // 2) : (k + 1) * (w // 2)] = updated[
                    :, q * (w // 2) : (q + 1) * (w // 2)
                ]

    def quantize(k):
        for h in range(2):
            for b in range(nb):
                j = h * hb + k * nb + b
                cols = pl.ds(j * BLOCK, BLOCK)
                first, second = fbase[:, cols], sbase[:, cols]
                peak = jnp.max(jnp.abs(first), axis=1, keepdims=True) + scale_eps
                new_fs[:, j : j + 1] = peak
                new_first[:, cols] = (first / peak).astype(bf16)
                peak = jnp.max(second, axis=1, keepdims=True) + scale_eps
                new_ss[:, j : j + 1] = peak
                new_second[:, cols] = (second / peak).astype(bf16)

    per = CHUNKS // GROUPS
    wide = per * (w // 2)
    locals_ = []

    def place(e, zz, yy, xx, lo=0, width=wide):
        row = pl.multiple_of(index(zz, yy, xx, c) * TILE, TILE)
        return comm.at[pl.ds(row, TILE), pl.ds(e * wide + lo, width)]

    def gather_own(e):
        cols = pl.ds(e * wide, wide)
        slot[:, cols] = slotf[:, cols].astype(bf16)
        src, dst = slot.at[:, cols], place(e, z, y, x)
        for d in range(1, 4):
            send(src, dst, az_sem, (e, d), zn[d])
        send(src, dst, ax_sem, (e, 0), xn)
        send(src, dst, ay_sem, (e, 0), yn)
        send(src, dst, as_sem, (e, 0), sibling)
        copy = pltpu.make_async_copy(src, dst, loc_sem.at[e])
        copy.start()
        locals_.append(copy)

    def gather_z(e):
        for d in range(1, 4):
            ref = place(e, z_from[d], y, x)
            remote(ref, ref, az_sem, (e, d), zn[d]).wait_recv()
            send(ref, ref, ax_sem, (e, d), xn)
            send(ref, ref, ay_sem, (e, d), yn)
            send(ref, ref, as_sem, (e, d), sibling)

    def gather_xy(e):
        for d in range(4):
            ref = place(e, z_from[d], y, 1 - x)
            remote(ref, ref, ax_sem, (e, d), xn).wait_recv()
            right = place(e, z_from[d], y, 1 - x, wide // 2, wide // 2)
            send(right, right, fy_sem, (e, d), yn)
            send(ref, ref, as_sem, (e, 4 + d), sibling)
            ref = place(e, z_from[d], 1 - y, x)
            remote(ref, ref, ay_sem, (e, d), yn).wait_recv()
            left = place(e, z_from[d], 1 - y, x, 0, wide // 2)
            send(left, left, fx_sem, (e, d), xn)
            send(ref, ref, as_sem, (e, 8 + d), sibling)

    def gather_far(e):
        for d in range(4):
            ref = place(e, z_from[d], 1 - y, 1 - x)
            left = place(e, z_from[d], 1 - y, 1 - x, 0, wide // 2)
            right = place(e, z_from[d], 1 - y, 1 - x, wide // 2, wide // 2)
            remote(left, left, fx_sem, (e, d), xn).wait_recv()
            remote(right, right, fy_sem, (e, d), yn).wait_recv()
            send(ref, ref, as_sem, (e, 12 + d), sibling)

    def gather_end(e):
        for q in range(4):
            for d in range(4):
                yy = 1 - y if q >= 2 else y
                xx = 1 - x if q % 2 == 1 else x
                row = pl.multiple_of(index(z_from[d], yy, xx, 1 - c) * TILE, TILE)
                ref = comm.at[pl.ds(row, TILE), pl.ds(e * wide, wide)]
                remote(ref, ref, as_sem, (e, 4 * q + d), sibling).wait_recv()

    for k in range(CHUNKS):
        core_sum(k)
    for k in range(CHUNKS):
        base(k)
    for k in range(CHUNKS):
        first_axis(k)
    for k in range(CHUNKS):
        second_axis(k)
    for e in range(GROUPS):
        ks = range(e * per, (e + 1) * per)
        for k in ks:
            along_z(k)
        for k in ks:
            adam(k)
        gather_own(e)
        if e < GROUPS - 1:
            for k in ks:
                quantize(k)
    for e in range(GROUPS):
        gather_z(e)
    for k in range((GROUPS - 1) * per, CHUNKS):
        quantize(k)
    for e in range(GROUPS):
        gather_xy(e)
    for e in range(GROUPS):
        gather_far(e)
    for e in range(GROUPS):
        gather_end(e)
    for copy in sent:
        copy.wait_send()
    for copy in locals_:
        copy.wait()


def exchange(grad, gscale, master, fm, fs, sm, ss):
    rows, d = grad.shape
    own_rows = master.shape[0]
    w = d // 2 // CHUNKS
    K, G = CHUNKS, GROUPS
    vmem = pl.BlockSpec(memory_space=pltpu.VMEM)
    dma = pltpu.SemaphoreType.DMA
    return pl.pallas_call(
        exchange_kernel,
        out_shape=(
            jax.ShapeDtypeStruct((rows * 4, d // 4), bf16),
            jax.ShapeDtypeStruct(master.shape, f32),
            jax.ShapeDtypeStruct(fm.shape, bf16),
            jax.ShapeDtypeStruct(fs.shape, f32),
            jax.ShapeDtypeStruct(sm.shape, bf16),
            jax.ShapeDtypeStruct(ss.shape, f32),
        ),
        in_specs=[pl.BlockSpec(memory_space=pl.ANY)] + [vmem] * 6,
        out_specs=(pl.BlockSpec(memory_space=pl.ANY),) + (vmem,) * 5,
        scratch_shapes=[
            pltpu.VMEM((K, rows, w), bf16),
            pltpu.VMEM((K, rows, w), bf16),
            pltpu.VMEM(gscale.shape, bf16),
            pltpu.VMEM((rows, gscale.shape[1] // 2), f32),
            pltpu.VMEM((rows, gscale.shape[1] // 2), f32),
            pltpu.VMEM((K, 2, 2, 4, 8, w), f32),
            pltpu.VMEM((K, 2, 4, 8, w), f32),
            pltpu.VMEM((K, 4, 8, w), f32),
            pltpu.VMEM((K, 4, 8, w), f32),
            pltpu.VMEM((K, 4, 8, w), f32),
            pltpu.VMEM((2, K, 8, w), f32),
            pltpu.VMEM((own_rows, d), f32),
            pltpu.VMEM((own_rows, d), f32),
            pltpu.VMEM((TILE, d // 4), f32),
            pltpu.VMEM((TILE, d // 4), bf16),
            dma((K,)),
            dma((2, 1)),
            dma((2, K)),
            dma((2, K)),
            dma((2, K)),
            dma((2, K, 4)),
            dma((2, K)),
            dma((2, G, 4)),
            dma((2, G, 4)),
            dma((2, G, 4)),
            dma((2, G, 4)),
            dma((2, G, 4)),
            dma((2, G, 16)),
            dma((G,)),
        ],
        compiler_params=pltpu.CompilerParams(
            collective_id=0, has_side_effects=True, vmem_limit_bytes=40 * 1024 * 1024
        ),
        cost_estimate=pl.CostEstimate(
            flops=8 * rows * d, bytes_accessed=8 * rows * d, transcendentals=own_rows * d
        ),
        name="exchange",
    )(grad, gscale, master, fm, fs, sm, ss)


def assemble_kernel(comm, *refs):
    smalls, (weights, transposed), copied = refs[:5], refs[5:7], refs[7:12]
    sem = refs[12]
    t = pl.program_id(0) * 4 + pl.program_id(1)
    last = pl.num_programs(0) * 4 - 1
    copies = [pltpu.make_async_copy(a, b, sem.at[i]) for i, (a, b) in enumerate(zip(smalls, copied))]

    @pl.when(t == 0)
    def _():
        for copy in copies:
            copy.start()

    rows, cols = weights.shape
    kk = pl.program_id(1)
    row = lax.broadcasted_iota(jnp.int32, (rows, rows * 4), 0)
    col = lax.broadcasted_iota(jnp.int32, (rows, rows * 4), 1)
    wanted = (row // 4) * TILE + 4 * kk + lax.rem(row, 4)
    pick = jnp.where(col == wanted, 1.0, 0.0).astype(bf16)
    w = jnp.dot(pick, comm[...], preferred_element_type=f32).astype(bf16)
    weights[...] = w
    step = 256
    eye = jnp.where(
        lax.broadcasted_iota(jnp.int32, (step, step), 0)
        == lax.broadcasted_iota(jnp.int32, (step, step), 1),
        1.0,
        0.0,
    ).astype(bf16)
    for i in range(cols // step):
        turned = lax.dot_general(
            eye,
            w[:, i * step : (i + 1) * step],
            (((1,), (1,)), ((), ())),
            preferred_element_type=f32,
        )
        transposed[i * step : (i + 1) * step, :] = turned.astype(bf16)

    @pl.when(t == last)
    def _():
        for copy in copies:
            copy.wait()


def assemble(comm, smalls):
    rows = comm.shape[0] // 4
    d = comm.shape[1] * 4
    cols = d // 4 // CHUNKS
    anywhere = pl.BlockSpec(memory_space=pl.ANY)

    def column(k, kk):
        return (kk // 2) * (2 * CHUNKS) + 2 * k + lax.rem(kk, 2)

    return pl.pallas_call(
        assemble_kernel,
        grid=(CHUNKS, 4),
        out_shape=(
            jax.ShapeDtypeStruct((rows, d), bf16),
            jax.ShapeDtypeStruct((d, rows), bf16),
        )
        + tuple(jax.ShapeDtypeStruct(s.shape, s.dtype) for s in smalls),
        in_specs=[pl.BlockSpec((rows * 4, cols), lambda k, kk: (0, k))] + [anywhere] * 5,
        out_specs=(
            pl.BlockSpec((rows, cols), lambda k, kk: (0, column(k, kk))),
            pl.BlockSpec((cols, rows), lambda k, kk: (column(k, kk), 0)),
        )
        + (anywhere,) * 5,
        scratch_shapes=[pltpu.SemaphoreType.DMA((5,))],
        compiler_params=pltpu.CompilerParams(
            vmem_limit_bytes=32 * 1024 * 1024,
            dimension_semantics=("arbitrary", "arbitrary"),
        ),
        name="assemble",
    )(comm, *smalls)


def fused_on_device(
    grad_values, grad_scales, master, first_moment, first_scale, second_moment, second_scale
):
    def flat(array):
        return array.reshape(array.shape[-2:])

    comm, *smalls = exchange(
        flat(grad_values),
        flat(grad_scales),
        flat(master),
        flat(first_moment),
        flat(first_scale),
        flat(second_moment),
        flat(second_scale),
    )
    weights, transposed, *smalls = assemble(comm, smalls)
    return tuple(array[None] for array in (*smalls, weights, transposed))


def expand(values, scales):
    shape = values.shape
    blocks = values.astype(f32).reshape(shape[:-1] + (shape[-1] // BLOCK, BLOCK))
    return (blocks * scales.astype(f32)[..., None]).reshape(shape)


def quantize_blocks(values, signed):
    shape = values.shape
    blocks = values.reshape(shape[:-1] + (shape[-1] // BLOCK, BLOCK))
    if signed:
        peak = jnp.max(jnp.abs(blocks), axis=-1) + scale_eps
    else:
        peak = jnp.max(blocks, axis=-1) + scale_eps
    coded = (blocks / peak[..., None]).astype(bf16).reshape(shape)
    return (coded, peak)


def adam_step(gradient, master, first_moment, first_scale, second_moment, second_scale):
    first = beta_one * expand(first_moment, first_scale) + (1.0 - beta_one) * gradient
    second = beta_two * expand(second_moment, second_scale) + (1.0 - beta_two) * gradient * gradient
    direction = first / corr_one / (jnp.sqrt(second / corr_two) + adam_eps)
    updated = master - rate * direction
    first_coded, first_peak = quantize_blocks(first, True)
    second_coded, second_peak = quantize_blocks(second, False)
    return (updated, first_coded, first_peak, second_coded, second_peak, updated.astype(bf16))


def on_device(
    grad_values, grad_scales, master, first_moment, first_scale, second_moment, second_scale
):
    arrived, arrived_scales = (
        lax.all_to_all(grad_values, "group", split_axis=3, concat_axis=1, tiled=True),
        lax.all_to_all(grad_scales, "group", split_axis=3, concat_axis=1, tiled=True),
    )
    partial_sum = jnp.sum(expand(arrived, arrived_scales), axis=1)
    partial_sum = partial_sum.reshape(master.shape)
    gradient = lax.psum(partial_sum, "node")
    result = adam_step(gradient, master, first_moment, first_scale, second_moment, second_scale)
    updated, first_coded, first_peak, second_coded, second_peak, low_weights = result
    weights = lax.all_gather(low_weights, "group", axis=1, tiled=True)
    transposed = jnp.swapaxes(weights, 1, 2)
    return (updated, first_coded, first_peak, second_coded, second_peak, weights, transposed)


def solution(mesh):
    placed = (
        P("node", "group", "fsdp", None, None),
        P("node", "group", "fsdp", None, None),
        P("fsdp", "group", None),
        P("fsdp", "group", None),
        P("fsdp", "group", None),
        P("fsdp", "group", None),
        P("fsdp", "group", None),
    )
    fused = mesh.shape["node"] == 1 and mesh.shape["group"] == 32
    return jax.shard_map(
        fused_on_device if fused else on_device,
        mesh=mesh,
        in_specs=placed,
        out_specs=(
            P("fsdp", "group", None),
            P("fsdp", "group", None),
            P("fsdp", "group", None),
            P("fsdp", "group", None),
            P("fsdp", "group", None),
            P("fsdp", None, None),
            P("fsdp", None, None),
        ),
        check_vma=False,
    )
```

```python
import functools

import jax
import jax.numpy as jnp
from jax import lax
from jax.experimental import pallas as pl
from jax.experimental.pallas import tpu as pltpu
from jax.sharding import PartitionSpec as P

BLOCK = 128
CHUNKS = 8
GROUPS = 4
TILE = 16

beta_one = 0.9
beta_two = 0.95
rate = 0.02
adam_eps = 1e-08
scale_eps = 1e-06
corr_one = 1.0 - 0.9**10
corr_two = 1.0 - 0.95**10

f32 = jnp.float32
bf16 = jnp.bfloat16


def exchange_kernel(
    grad, gscale, master_in, fm_in, fs_in, sm_in, ss_in,
    comm, master_out, first_out, fs_out, second_out, ss_out,
    own, sib, sc_own, sc_sib, sh_own, sh_sib, part, rx1, rx2, acc, rx3, gfull, fbase, sbase, slotf, slot,
    master, fm, fs, sm, ss, new_master, new_first, new_fs, new_second, new_ss,
    in_sem, out_sem, own_sem, sc_sem, sib_sem, p1_sem, p2_sem, z_sem, g_sem,
    az_sem, ax_sem, ay_sem, fx_sem, fy_sem, as_sem, loc_sem,
):
    w = grad.shape[1] // 2 // CHUNKS
    nb = w // BLOCK
    me = lax.axis_index("group")
    c = lax.rem(me, 2)
    x = lax.rem(me // 2, 2)
    y = lax.rem(me // 4, 2)
    z = me // 8

    def index(zz, yy, xx, cc):
        return zz * 8 + yy * 4 + xx * 2 + cc

    sibling = index(z, y, x, 1 - c)
    xn = index(z, y, 1 - x, c)
    yn = index(z, 1 - y, x, c)
    z_up = [lax.rem(z + d, 4) for d in range(4)]
    z_from = [lax.rem(z + 4 - d, 4) for d in range(4)]
    zn = [index(z_up[d], y, x, c) for d in range(4)]

    def remote(src, dst, sems, at, to):
        return pltpu.make_async_remote_copy(
            src_ref=src,
            dst_ref=dst,
            send_sem=sems.at[(0,) + at],
            recv_sem=sems.at[(1,) + at],
            device_id={"group": to},
            device_id_type=pl.DeviceIdType.MESH,
        )

    sent = []

    def send(*args):
        copy = remote(*args)
        copy.start()
        sent.append(copy)
        return copy

    def local(src, dst, sem):
        copy = pltpu.make_async_copy(src, dst, sem)
        copy.start()
        return copy

    def columns(k, h):
        return k * 2 * w + h * w

    scale_own = local(gscale, sc_own, in_sem.at[5])
    own_copies = []
    for k in range(CHUNKS):
        here = pl.multiple_of(columns(k, c), BLOCK)
        own_copies.append(local(grad.at[:, pl.ds(here, w)], own.at[k], own_sem.at[k]))

    barrier = pltpu.get_barrier_semaphore()
    partners = [sibling, xn, yn] + zn[1:]
    for to in partners:
        pl.semaphore_signal(
            barrier, inc=1, device_id={"group": to}, device_id_type=pl.DeviceIdType.MESH
        )
    pl.semaphore_wait(barrier, len(partners))

    scale_copy = send(gscale, sc_sib, sc_sem, (0,), sibling)
    sib_copies = []
    for k in range(CHUNKS):
        there = pl.multiple_of(columns(k, 1 - c), BLOCK)
        sib_copies.append(send(grad.at[:, pl.ds(there, w)], sib.at[k], sib_sem, (k,), sibling))
    fetched = [
        local(src, dst, in_sem.at[i])
        for i, (src, dst) in enumerate(
            ((fm_in, fm), (fs_in, fs), (sm_in, sm), (ss_in, ss), (master_in, master))
        )
    ]

    def half_scales(ref, out):
        values = ref[...].astype(f32)
        for k in range(CHUNKS):
            j = 2 * k * nb
            out[:, k * nb : (k + 1) * nb] = jnp.where(
                c == 0, values[:, j : j + nb], values[:, j + nb : j + 2 * nb]
            )

    scale_own.wait()
    half_scales(sc_own, sh_own)
    scale_copy.wait_recv()
    half_scales(sc_sib, sh_sib)

    def order(k):
        return (x, y, xn, yn) if k % 2 == 0 else (y, x, yn, xn)

    p1, p2 = {}, {}

    def core_sum(k):
        own_copies[k].wait()
        sib_copies[k].wait_recv()

        def body(i, carry):
            rows = pl.ds(pl.multiple_of(i * 16, 16), 16)
            so, sb = sh_own[rows, :], sh_sib[rows, :]
            zz, yy = i // 2, lax.rem(i, 2)
            for b in range(nb):
                j = k * nb + b
                cols = pl.ds(b * BLOCK, BLOCK)
                v = own[k, rows, cols].astype(f32) * so[:, j : j + 1]
                v += sib[k, rows, cols].astype(f32) * sb[:, j : j + 1]
                for xx in range(2):
                    one, two = (xx, yy) if k % 2 == 0 else (yy, xx)
                    part[k, one, two, zz, :, cols] = v[8 * xx : 8 * xx + 8]
            return carry

        lax.fori_loop(0, 8, body, 0)
        a, _, an, _ = order(k)
        p1[k] = send(part.at[k, 1 - a], rx1.at[k], p1_sem, (k,), an)

    def base(k):
        for b in range(2 * nb):
            j = 2 * k * nb + b
            cols = pl.ds(j * BLOCK, BLOCK)
            fbase[:, cols] = beta_one * (fm[:, cols].astype(f32) * fs[:, j : j + 1])
            sbase[:, cols] = beta_two * (sm[:, cols].astype(f32) * ss[:, j : j + 1])

    def first_axis(k):
        a, b, _, bn = order(k)
        p1[k].wait_recv()
        for zz in range(4):
            part[k, a, 1 - b, zz] = part[k, a, 1 - b, zz] + rx1[k, 1 - b, zz]
        p2[k] = send(part.at[k, a, 1 - b], rx2.at[k], p2_sem, (k,), bn)

    def second_axis(k):
        a, b, _, _ = order(k)
        p2[k].wait_recv()
        for zz in range(4):
            acc[k, zz] = part[k, a, b, zz] + rx1[k, b, zz] + rx2[k, zz]
        for d in range(1, 4):
            send(acc.at[k, z_up[d]], rx3.at[k, d], z_sem, (k, d), zn[d])

    def along_z(k):
        total = acc[k, z]
        for d in range(1, 4):
            remote(acc.at[k, z_up[d]], rx3.at[k, d], z_sem, (k, d), zn[d]).wait_recv()
            total = total + rx3[k, d]
        gfull[c, k] = total
        send(gfull.at[c, k], gfull.at[c, k], g_sem, (k,), sibling)

    def adam(k):
        remote(gfull.at[1 - c, k], gfull.at[1 - c, k], g_sem, (k,), sibling).wait_recv()
        for h in range(2):
            cols = pl.ds(columns(k, h), w)
            v = gfull[h, k]
            g = jnp.where(c == 0, v[0:4], v[4:8])
            first = fbase[:, cols] + (1.0 - beta_one) * g
            second = sbase[:, cols] + (1.0 - beta_two) * g * g
            fbase[:, cols] = first
            sbase[:, cols] = second
            direction = first / corr_one / (jnp.sqrt(second / corr_two) + adam_eps)
            updated = master[:, cols] - rate * direction
            new_master[:, cols] = updated
            for q in range(2):
                r = 4 * (2 * h + q)
                slotf[r : r + 4, k * (w // 2) : (k + 1) * (w // 2)] = updated[
                    :, q * (w // 2) : (q + 1) * (w // 2)
                ]

    def quantize(k):
        for b in range(2 * nb):
            j = 2 * k * nb + b
            cols = pl.ds(j * BLOCK, BLOCK)
            first, second = fbase[:, cols], sbase[:, cols]
            peak = jnp.max(jnp.abs(first), axis=1, keepdims=True) + scale_eps
            new_fs[:, j : j + 1] = peak
            new_first[:, cols] = (first / peak).astype(bf16)
            peak = jnp.max(second, axis=1, keepdims=True) + scale_eps
            new_ss[:, j : j + 1] = peak
            new_second[:, cols] = (second / peak).astype(bf16)

    per = CHUNKS // GROUPS
    wide = per * (w // 2)
    half = wide // 2
    placed = []

    def place(e, yy, xx, cc, zz=None, lo=0, width=wide):
        row = pl.multiple_of(index(0, yy, xx, cc) * 4 * TILE, TILE)
        count = 4 * TILE
        if zz is not None:
            row, count = pl.multiple_of(row + zz * TILE, TILE), TILE
        return comm.at[pl.ds(row, count), pl.ds(e * wide + lo, width)]

    def gather_own(e):
        cols = pl.ds(e * wide, wide)
        slot[:, cols] = slotf[:, cols].astype(bf16)
        src, dst = slot.at[:, cols], place(e, y, x, c, z)
        for d in range(1, 4):
            send(src, dst, az_sem, (e, d), zn[d])
        placed.append(local(src, dst, loc_sem.at[e]))

    def gather_z(e):
        placed[e].wait()
        for d in range(1, 4):
            ref = place(e, y, x, c, z_from[d])
            remote(ref, ref, az_sem, (e, d), zn[d]).wait_recv()
        ref = place(e, y, x, c)
        send(ref, ref, ax_sem, (e,), xn)
        send(ref, ref, ay_sem, (e,), yn)
        send(ref, ref, as_sem, (e, 0), sibling)

    def gather_xy(e):
        ref = place(e, y, 1 - x, c)
        remote(ref, ref, ax_sem, (e,), xn).wait_recv()
        right = place(e, y, 1 - x, c, None, half, half)
        send(right, right, fy_sem, (e,), yn)
        other = place(e, 1 - y, x, c)
        remote(other, other, ay_sem, (e,), yn).wait_recv()
        left = place(e, 1 - y, x, c, None, 0, half)
        send(left, left, fx_sem, (e,), xn)
        send(ref, ref, as_sem, (e, 1), sibling)
        send(other, other, as_sem, (e, 2), sibling)

    def gather_far(e):
        left = place(e, 1 - y, 1 - x, c, None, 0, half)
        right = place(e, 1 - y, 1 - x, c, None, half, half)
        remote(left, left, fx_sem, (e,), xn).wait_recv()
        remote(right, right, fy_sem, (e,), yn).wait_recv()
        ref = place(e, 1 - y, 1 - x, c)
        send(ref, ref, as_sem, (e, 3), sibling)

    def gather_end(e):
        for q in range(4):
            yy = 1 - y if q >= 2 else y
            xx = 1 - x if q % 2 == 1 else x
            ref = place(e, yy, xx, 1 - c)
            remote(ref, ref, as_sem, (e, q), sibling).wait_recv()

    def chunks(e):
        return range(e * per, (e + 1) * per)

    def bases(e):
        for k in chunks(e):
            base(k)

    def step(e):
        for k in chunks(e):
            along_z(k)
        for k in chunks(e):
            adam(k)
        gather_own(e)
        for k in chunks(e):
            quantize(k)

    for e in range(2):
        for k in chunks(e):
            core_sum(k)
    for copy in fetched:
        copy.wait()
    bases(0)
    bases(1)
    for t in range(1, GROUPS + 6):
        if t - 1 < GROUPS:
            for k in chunks(t - 1):
                first_axis(k)
        if t + 1 < GROUPS:
            for k in chunks(t + 1):
                core_sum(k)
            bases(t + 1)
        if 0 <= t - 2 < GROUPS:
            for k in chunks(t - 2):
                second_axis(k)
        if 0 <= t - 3 < GROUPS:
            step(t - 3)
        if 0 <= t - 4 < GROUPS:
            gather_z(t - 4)
        if 0 <= t - 5 < GROUPS:
            gather_xy(t - 5)
        if 0 <= t - 6 < GROUPS:
            gather_far(t - 6)
    stored = [
        local(src, dst, out_sem.at[i])
        for i, (src, dst) in enumerate(
            (
                (new_master, master_out),
                (new_first, first_out),
                (new_fs, fs_out),
                (new_second, second_out),
                (new_ss, ss_out),
            )
        )
    ]
    for e in range(GROUPS):
        gather_end(e)
    for copy in sent:
        copy.wait_send()
    for copy in stored:
        copy.wait()


def exchange(grad, gscale, master, fm, fs, sm, ss):
    rows, d = grad.shape
    own_rows = master.shape[0]
    w = d // 2 // CHUNKS
    K, G = CHUNKS, GROUPS
    anywhere = pl.BlockSpec(memory_space=pl.ANY)
    dma = pltpu.SemaphoreType.DMA
    smalls = (master, fm, fs, sm, ss)
    return pl.pallas_call(
        exchange_kernel,
        out_shape=(jax.ShapeDtypeStruct((rows * 4, d // 4), bf16),)
        + tuple(jax.ShapeDtypeStruct(s.shape, s.dtype) for s in smalls),
        in_specs=[anywhere] * 7,
        out_specs=(anywhere,) * 6,
        scratch_shapes=[
            pltpu.VMEM((K, rows, w), bf16),
            pltpu.VMEM((K, rows, w), bf16),
            pltpu.VMEM(gscale.shape, bf16),
            pltpu.VMEM(gscale.shape, bf16),
            pltpu.VMEM((rows, gscale.shape[1] // 2), f32),
            pltpu.VMEM((rows, gscale.shape[1] // 2), f32),
            pltpu.VMEM((K, 2, 2, 4, 8, w), f32),
            pltpu.VMEM((K, 2, 4, 8, w), f32),
            pltpu.VMEM((K, 4, 8, w), f32),
            pltpu.VMEM((K, 4, 8, w), f32),
            pltpu.VMEM((K, 4, 8, w), f32),
            pltpu.VMEM((2, K, 8, w), f32),
            pltpu.VMEM((own_rows, d), f32),
            pltpu.VMEM((own_rows, d), f32),
            pltpu.VMEM((TILE, d // 4), f32),
            pltpu.VMEM((TILE, d // 4), bf16),
        ]
        + [pltpu.VMEM(s.shape, s.dtype) for s in smalls + smalls]
        + [
            dma((6,)),
            dma((5,)),
            dma((K,)),
            dma((2, 1)),
            dma((2, K)),
            dma((2, K)),
            dma((2, K)),
            dma((2, K, 4)),
            dma((2, K)),
            dma((2, G, 4)),
            dma((2, G)),
            dma((2, G)),
            dma((2, G)),
            dma((2, G)),
            dma((2, G, 4)),
            dma((G,)),
        ],
        compiler_params=pltpu.CompilerParams(
            collective_id=0, has_side_effects=True, vmem_limit_bytes=60 * 1024 * 1024
        ),
        cost_estimate=pl.CostEstimate(
            flops=8 * rows * d, bytes_accessed=8 * rows * d, transcendentals=own_rows * d
        ),
        name="exchange",
    )(grad, gscale, master, fm, fs, sm, ss)


def assemble_kernel(comm, *refs):
    smalls, (weights, transposed), copied = refs[:5], refs[5:7], refs[7:12]
    pick, eye, sem = refs[12:]
    t = pl.program_id(0)
    rows = weights.shape[0]
    cols = comm.shape[1]
    step = eye.shape[0]
    copies = [pltpu.make_async_copy(a, b, sem.at[i]) for i, (a, b) in enumerate(zip(smalls, copied))]

    @pl.when(t == 0)
    def _():
        for copy in copies:
            copy.start()
        row = lax.broadcasted_iota(jnp.int32, pick.shape, 0)
        col = lax.broadcasted_iota(jnp.int32, pick.shape, 1)
        kk, r = row // rows, lax.rem(row, rows)
        device = r // 4
        wanted = (lax.rem(device, 8) * 4 + device // 8) * TILE + 4 * kk + lax.rem(r, 4)
        pick[...] = jnp.where(col == wanted, 1.0, 0.0).astype(bf16)
        row = lax.broadcasted_iota(jnp.int32, eye.shape, 0)
        col = lax.broadcasted_iota(jnp.int32, eye.shape, 1)
        eye[...] = jnp.where(row == col, 1.0, 0.0).astype(bf16)

    sorted_rows = jnp.dot(pick[...], comm[...], preferred_element_type=f32).astype(bf16)
    for kk in range(4):
        weights[:, kk * cols : (kk + 1) * cols] = sorted_rows[kk * rows : (kk + 1) * rows]
    for i in range(4 * cols // step):
        turned = lax.dot_general(
            eye[...],
            weights[:, i * step : (i + 1) * step],
            (((1,), (1,)), ((), ())),
            preferred_element_type=f32,
        )
        transposed[i * step : (i + 1) * step, :] = turned.astype(bf16)

    @pl.when(t == pl.num_programs(0) - 1)
    def _():
        for copy in copies:
            copy.wait()


def assemble(comm, smalls):
    rows = comm.shape[0] // 4
    d = comm.shape[1] * 4
    cols = d // 4 // CHUNKS
    anywhere = pl.BlockSpec(memory_space=pl.ANY)
    return pl.pallas_call(
        assemble_kernel,
        grid=(CHUNKS,),
        out_shape=(
            jax.ShapeDtypeStruct((rows, d), bf16),
            jax.ShapeDtypeStruct((d, rows), bf16),
        )
        + tuple(jax.ShapeDtypeStruct(s.shape, s.dtype) for s in smalls),
        in_specs=[pl.BlockSpec((rows * 4, cols), lambda k: (0, k))] + [anywhere] * 5,
        out_specs=(
            pl.BlockSpec((rows, 4 * cols), lambda k: (0, k)),
            pl.BlockSpec((4 * cols, rows), lambda k: (k, 0)),
        )
        + (anywhere,) * 5,
        scratch_shapes=[
            pltpu.VMEM((rows * 4, rows * 4), bf16),
            pltpu.VMEM((256, 256), bf16),
            pltpu.SemaphoreType.DMA((5,)),
        ],
        compiler_params=pltpu.CompilerParams(
            vmem_limit_bytes=60 * 1024 * 1024,
            dimension_semantics=("arbitrary",),
        ),
        name="assemble",
    )(comm, *smalls)


def fused_on_device(
    grad_values, grad_scales, master, first_moment, first_scale, second_moment, second_scale
):
    def flat(array):
        return array.reshape(array.shape[-2:])

    comm, *smalls = exchange(
        flat(grad_values),
        flat(grad_scales),
        flat(master),
        flat(first_moment),
        flat(first_scale),
        flat(second_moment),
        flat(second_scale),
    )
    weights, transposed, *smalls = assemble(comm, smalls)
    return tuple(array[None] for array in (*smalls, weights, transposed))


def expand(values, scales):
    shape = values.shape
    blocks = values.astype(f32).reshape(shape[:-1] + (shape[-1] // BLOCK, BLOCK))
    return (blocks * scales.astype(f32)[..., None]).reshape(shape)


def quantize_blocks(values, signed):
    shape = values.shape
    blocks = values.reshape(shape[:-1] + (shape[-1] // BLOCK, BLOCK))
    if signed:
        peak = jnp.max(jnp.abs(blocks), axis=-1) + scale_eps
    else:
        peak = jnp.max(blocks, axis=-1) + scale_eps
    coded = (blocks / peak[..., None]).astype(bf16).reshape(shape)
    return (coded, peak)


def adam_step(gradient, master, first_moment, first_scale, second_moment, second_scale):
    first = beta_one * expand(first_moment, first_scale) + (1.0 - beta_one) * gradient
    second = beta_two * expand(second_moment, second_scale) + (1.0 - beta_two) * gradient * gradient
    direction = first / corr_one / (jnp.sqrt(second / corr_two) + adam_eps)
    updated = master - rate * direction
    first_coded, first_peak = quantize_blocks(first, True)
    second_coded, second_peak = quantize_blocks(second, False)
    return (updated, first_coded, first_peak, second_coded, second_peak, updated.astype(bf16))


def on_device(
    grad_values, grad_scales, master, first_moment, first_scale, second_moment, second_scale
):
    arrived, arrived_scales = (
        lax.all_to_all(grad_values, "group", split_axis=3, concat_axis=1, tiled=True),
        lax.all_to_all(grad_scales, "group", split_axis=3, concat_axis=1, tiled=True),
    )
    partial_sum = jnp.sum(expand(arrived, arrived_scales), axis=1)
    partial_sum = partial_sum.reshape(master.shape)
    gradient = lax.psum(partial_sum, "node")
    result = adam_step(gradient, master, first_moment, first_scale, second_moment, second_scale)
    updated, first_coded, first_peak, second_coded, second_peak, low_weights = result
    weights = lax.all_gather(low_weights, "group", axis=1, tiled=True)
    transposed = jnp.swapaxes(weights, 1, 2)
    return (updated, first_coded, first_peak, second_coded, second_peak, weights, transposed)


def solution(mesh):
    placed = (
        P("node", "group", "fsdp", None, None),
        P("node", "group", "fsdp", None, None),
        P("fsdp", "group", None),
        P("fsdp", "group", None),
        P("fsdp", "group", None),
        P("fsdp", "group", None),
        P("fsdp", "group", None),
    )
    fused = mesh.shape["node"] == 1 and mesh.shape["group"] == 32
    return jax.shard_map(
        fused_on_device if fused else on_device,
        mesh=mesh,
        in_specs=placed,
        out_specs=(
            P("fsdp", "group", None),
            P("fsdp", "group", None),
            P("fsdp", "group", None),
            P("fsdp", "group", None),
            P("fsdp", "group", None),
            P("fsdp", None, None),
            P("fsdp", None, None),
        ),
        check_vma=False,
    )
```

```python
import functools

import jax
import jax.numpy as jnp
from jax import lax
from jax.experimental import pallas as pl
from jax.experimental.pallas import tpu as pltpu
from jax.sharding import PartitionSpec as P

BLOCK = 128
CHUNKS = 8
GROUPS = 4
TILE = 16

beta_one = 0.9
beta_two = 0.95
rate = 0.02
adam_eps = 1e-08
scale_eps = 1e-06
corr_one = 1.0 - 0.9**10
corr_two = 1.0 - 0.95**10

f32 = jnp.float32
bf16 = jnp.bfloat16


def exchange_kernel(
    grad, gscale, master_in, fm_in, fs_in, sm_in, ss_in,
    comm, master_out, first_out, fs_out, second_out, ss_out,
    own, sib, sc_own, sc_sib, sh_own, sh_sib, part, rx1, rx2, acc, rx3, gfull, fbase, sbase, slotf, slot, held,
    master, fm, fs, sm, ss, new_master, new_first, new_fs, new_second, new_ss,
    in_sem, out_sem, own_sem, sc_sem, sib_sem, p1_sem, p2_sem, z_sem, g_sem,
    az_sem, ax_sem, ay_sem, fx_sem, fy_sem, as_sem, loc_sem,
):
    w = grad.shape[1] // 2 // CHUNKS
    nb = w // BLOCK
    me = lax.axis_index("group")
    c = lax.rem(me, 2)
    x = lax.rem(me // 2, 2)
    y = lax.rem(me // 4, 2)
    z = me // 8

    def index(zz, yy, xx, cc):
        return zz * 8 + yy * 4 + xx * 2 + cc

    sibling = index(z, y, x, 1 - c)
    xn = index(z, y, 1 - x, c)
    yn = index(z, 1 - y, x, c)
    z_up = [lax.rem(z + d, 4) for d in range(4)]
    z_from = [lax.rem(z + 4 - d, 4) for d in range(4)]
    zn = [index(z_up[d], y, x, c) for d in range(4)]

    def remote(src, dst, sems, at, to):
        return pltpu.make_async_remote_copy(
            src_ref=src,
            dst_ref=dst,
            send_sem=sems.at[(0,) + at],
            recv_sem=sems.at[(1,) + at],
            device_id={"group": to},
            device_id_type=pl.DeviceIdType.MESH,
        )

    sent = []

    def send(*args):
        copy = remote(*args)
        copy.start()
        sent.append(copy)
        return copy

    def local(src, dst, sem):
        copy = pltpu.make_async_copy(src, dst, sem)
        copy.start()
        return copy

    def columns(k, h):
        return k * 2 * w + h * w

    scale_own = local(gscale, sc_own, in_sem.at[5])
    own_copies = []
    for k in range(CHUNKS):
        here = pl.multiple_of(columns(k, c), BLOCK)
        own_copies.append(local(grad.at[:, pl.ds(here, w)], own.at[k], own_sem.at[k]))

    barrier = pltpu.get_barrier_semaphore()
    partners = [sibling, xn, yn] + zn[1:]
    for to in partners:
        pl.semaphore_signal(
            barrier, inc=1, device_id={"group": to}, device_id_type=pl.DeviceIdType.MESH
        )
    pl.semaphore_wait(barrier, len(partners))

    scale_copy = send(gscale, sc_sib, sc_sem, (0,), sibling)
    sib_copies = []
    for k in range(CHUNKS):
        there = pl.multiple_of(columns(k, 1 - c), BLOCK)
        sib_copies.append(send(grad.at[:, pl.ds(there, w)], sib.at[k], sib_sem, (k,), sibling))
    fetched = [
        local(src, dst, in_sem.at[i])
        for i, (src, dst) in enumerate(
            ((fm_in, fm), (fs_in, fs), (sm_in, sm), (ss_in, ss), (master_in, master))
        )
    ]

    def half_scales(ref, out):
        values = ref[...].astype(f32).T
        for k in range(CHUNKS):
            j = 2 * k * nb
            out[:, k * nb : (k + 1) * nb] = jnp.where(
                c == 0, values[:, j : j + nb], values[:, j + nb : j + 2 * nb]
            )

    scale_own.wait()
    half_scales(sc_own, sh_own)
    scale_copy.wait_recv()
    half_scales(sc_sib, sh_sib)

    def order(k):
        return (x, y, xn, yn) if k % 2 == 0 else (y, x, yn, xn)

    p1, p2 = {}, {}

    def core_sum(k):
        own_copies[k].wait()
        sib_copies[k].wait_recv()

        def body(i, carry):
            rows = pl.ds(pl.multiple_of(i * 16, 16), 16)
            so, sb = sh_own[rows, :], sh_sib[rows, :]
            zz, yy = i // 2, lax.rem(i, 2)
            for b in range(nb):
                j = k * nb + b
                cols = pl.ds(b * BLOCK, BLOCK)
                v = own[k, rows, cols].astype(f32) * so[:, j : j + 1]
                v += sib[k, rows, cols].astype(f32) * sb[:, j : j + 1]
                for xx in range(2):
                    one, two = (xx, yy) if k % 2 == 0 else (yy, xx)
                    part[k, one, two, zz, :, cols] = v[8 * xx : 8 * xx + 8]
            return carry

        lax.fori_loop(0, 8, body, 0)
        a, _, an, _ = order(k)
        p1[k] = send(part.at[k, 1 - a], rx1.at[k], p1_sem, (k,), an)

    def base(k):
        for b in range(2 * nb):
            j = 2 * k * nb + b
            cols = pl.ds(j * BLOCK, BLOCK)
            fbase[:, cols] = beta_one * (fm[:, cols].astype(f32) * fs[:, j : j + 1])
            sbase[:, cols] = beta_two * (sm[:, cols].astype(f32) * ss[:, j : j + 1])

    def first_axis(k):
        a, b, _, bn = order(k)
        p1[k].wait_recv()
        for zz in range(4):
            part[k, a, 1 - b, zz] = part[k, a, 1 - b, zz] + rx1[k, 1 - b, zz]
        p2[k] = send(part.at[k, a, 1 - b], rx2.at[k], p2_sem, (k,), bn)

    def second_axis(k):
        a, b, _, _ = order(k)
        p2[k].wait_recv()
        for zz in range(4):
            acc[k, zz] = part[k, a, b, zz] + rx1[k, b, zz] + rx2[k, zz]
        for d in range(1, 4):
            send(acc.at[k, z_up[d]], rx3.at[k, d], z_sem, (k, d), zn[d])

    def along_z(k):
        total = acc[k, z]
        for d in range(1, 4):
            remote(acc.at[k, z_up[d]], rx3.at[k, d], z_sem, (k, d), zn[d]).wait_recv()
            total = total + rx3[k, d]
        gfull[c, k] = total
        send(gfull.at[c, k], gfull.at[c, k], g_sem, (k,), sibling)

    def adam(k):
        remote(gfull.at[1 - c, k], gfull.at[1 - c, k], g_sem, (k,), sibling).wait_recv()
        for h in range(2):
            cols = pl.ds(columns(k, h), w)
            v = gfull[h, k]
            g = jnp.where(c == 0, v[0:4], v[4:8])
            first = fbase[:, cols] + (1.0 - beta_one) * g
            second = sbase[:, cols] + (1.0 - beta_two) * g * g
            fbase[:, cols] = first
            sbase[:, cols] = second
            direction = first / corr_one / (jnp.sqrt(second / corr_two) + adam_eps)
            updated = master[:, cols] - rate * direction
            new_master[:, cols] = updated
            for q in range(2):
                r = 4 * (2 * h + q)
                slotf[r : r + 4, k * (w // 2) : (k + 1) * (w // 2)] = updated[
                    :, q * (w // 2) : (q + 1) * (w // 2)
                ]

    def quantize(k):
        for b in range(2 * nb):
            j = 2 * k * nb + b
            cols = pl.ds(j * BLOCK, BLOCK)
            first, second = fbase[:, cols], sbase[:, cols]
            peak = jnp.max(jnp.abs(first), axis=1, keepdims=True) + scale_eps
            new_fs[:, j : j + 1] = peak
            new_first[:, cols] = (first / peak).astype(bf16)
            peak = jnp.max(second, axis=1, keepdims=True) + scale_eps
            new_ss[:, j : j + 1] = peak
            new_second[:, cols] = (second / peak).astype(bf16)

    per = CHUNKS // GROUPS
    wide = per * (w // 2)
    half = wide // 2
    placed = []

    def place(e, yy, xx, cc, zz=None, lo=0, width=wide):
        row = pl.multiple_of(index(0, yy, xx, cc) * 4 * TILE, TILE)
        count = 4 * TILE
        if zz is not None:
            row, count = pl.multiple_of(row + zz * TILE, TILE), TILE
        return held.at[e, pl.ds(row, count), pl.ds(lo, width)]

    def gather_own(e):
        cols = pl.ds(e * wide, wide)
        slot[:, cols] = slotf[:, cols].astype(bf16)
        src, dst = slot.at[:, cols], place(e, y, x, c, z)
        for d in range(1, 4):
            send(src, dst, az_sem, (e, d), zn[d])
        placed.append(local(src, dst, loc_sem.at[e]))

    def gather_z(e):
        placed[e].wait()
        for d in range(1, 4):
            ref = place(e, y, x, c, z_from[d])
            remote(ref, ref, az_sem, (e, d), zn[d]).wait_recv()
        ref = place(e, y, x, c)
        send(ref, ref, ax_sem, (e,), xn)
        send(ref, ref, ay_sem, (e,), yn)
        send(ref, ref, as_sem, (e, 0), sibling)

    def gather_xy(e):
        ref = place(e, y, 1 - x, c)
        remote(ref, ref, ax_sem, (e,), xn).wait_recv()
        right = place(e, y, 1 - x, c, None, half, half)
        send(right, right, fy_sem, (e,), yn)
        other = place(e, 1 - y, x, c)
        remote(other, other, ay_sem, (e,), yn).wait_recv()
        left = place(e, 1 - y, x, c, None, 0, half)
        send(left, left, fx_sem, (e,), xn)
        send(ref, ref, as_sem, (e, 1), sibling)
        send(other, other, as_sem, (e, 2), sibling)

    def gather_far(e):
        left = place(e, 1 - y, 1 - x, c, None, 0, half)
        right = place(e, 1 - y, 1 - x, c, None, half, half)
        remote(left, left, fx_sem, (e,), xn).wait_recv()
        remote(right, right, fy_sem, (e,), yn).wait_recv()
        ref = place(e, 1 - y, 1 - x, c)
        send(ref, ref, as_sem, (e, 3), sibling)

    def gather_end(e):
        for q in range(4):
            yy = 1 - y if q >= 2 else y
            xx = 1 - x if q % 2 == 1 else x
            ref = place(e, yy, xx, 1 - c)
            remote(ref, ref, as_sem, (e, q), sibling).wait_recv()
        return local(held.at[e], comm.at[e], loc_sem.at[e])

    def chunks(e):
        return range(e * per, (e + 1) * per)

    def bases(e):
        for k in chunks(e):
            base(k)

    def step(e):
        for k in chunks(e):
            along_z(k)
        for k in chunks(e):
            adam(k)
        gather_own(e)

    for e in range(2):
        for k in chunks(e):
            core_sum(k)
    for copy in fetched:
        copy.wait()
    bases(0)
    bases(1)
    for t in range(1, GROUPS + 6):
        if t - 1 < GROUPS:
            for k in chunks(t - 1):
                first_axis(k)
        if t + 1 < GROUPS:
            for k in chunks(t + 1):
                core_sum(k)
            bases(t + 1)
        if 0 <= t - 2 < GROUPS:
            for k in chunks(t - 2):
                second_axis(k)
        if 0 <= t - 3 < GROUPS:
            step(t - 3)
        if 0 <= t - 4 < GROUPS:
            gather_z(t - 4)
        if 0 <= t - 5 < GROUPS:
            gather_xy(t - 5)
        if 0 <= t - 6 < GROUPS:
            gather_far(t - 6)
        if 0 <= t - 4 < GROUPS:
            for k in chunks(t - 4):
                quantize(k)
    stored = [
        local(src, dst, out_sem.at[i])
        for i, (src, dst) in enumerate(
            (
                (new_master, master_out),
                (new_first, first_out),
                (new_fs, fs_out),
                (new_second, second_out),
                (new_ss, ss_out),
            )
        )
    ]
    for e in range(GROUPS):
        stored.append(gather_end(e))
    for copy in sent:
        copy.wait_send()
    for copy in stored:
        copy.wait()


def exchange(grad, gscale, master, fm, fs, sm, ss):
    rows, d = grad.shape
    own_rows = master.shape[0]
    w = d // 2 // CHUNKS
    K, G = CHUNKS, GROUPS
    anywhere = pl.BlockSpec(memory_space=pl.ANY)
    dma = pltpu.SemaphoreType.DMA
    smalls = (master, fm, fs, sm, ss)
    return pl.pallas_call(
        exchange_kernel,
        out_shape=(jax.ShapeDtypeStruct((G, rows * 4, d // 4 // G), bf16),)
        + tuple(jax.ShapeDtypeStruct(s.shape, s.dtype) for s in smalls),
        in_specs=[anywhere] * 7,
        out_specs=(anywhere,) * 6,
        scratch_shapes=[
            pltpu.VMEM((K, rows, w), bf16),
            pltpu.VMEM((K, rows, w), bf16),
            pltpu.VMEM(gscale.shape, bf16),
            pltpu.VMEM(gscale.shape, bf16),
            pltpu.VMEM((rows, gscale.shape[0] // 2), f32),
            pltpu.VMEM((rows, gscale.shape[0] // 2), f32),
            pltpu.VMEM((K, 2, 2, 4, 8, w), f32),
            pltpu.VMEM((K, 2, 4, 8, w), f32),
            pltpu.VMEM((K, 4, 8, w), f32),
            pltpu.VMEM((K, 4, 8, w), f32),
            pltpu.VMEM((K, 4, 8, w), f32),
            pltpu.VMEM((2, K, 8, w), f32),
            pltpu.VMEM((own_rows, d), f32),
            pltpu.VMEM((own_rows, d), f32),
            pltpu.VMEM((TILE, d // 4), f32),
            pltpu.VMEM((TILE, d // 4), bf16),
            pltpu.VMEM((G, rows * 4, d // 4 // G), bf16),
        ]
        + [pltpu.VMEM(s.shape, s.dtype) for s in smalls + smalls]
        + [
            dma((6,)),
            dma((5,)),
            dma((K,)),
            dma((2, 1)),
            dma((2, K)),
            dma((2, K)),
            dma((2, K)),
            dma((2, K, 4)),
            dma((2, K)),
            dma((2, G, 4)),
            dma((2, G)),
            dma((2, G)),
            dma((2, G)),
            dma((2, G)),
            dma((2, G, 4)),
            dma((G,)),
        ],
        compiler_params=pltpu.CompilerParams(
            collective_id=0, has_side_effects=True, vmem_limit_bytes=60 * 1024 * 1024
        ),
        cost_estimate=pl.CostEstimate(
            flops=8 * rows * d, bytes_accessed=8 * rows * d, transcendentals=own_rows * d
        ),
        name="exchange",
    )(grad, gscale, master, fm, fs, sm, ss)


def assemble_kernel(comm, *refs):
    smalls, (weights, transposed), copied = refs[:5], refs[5:7], refs[7:12]
    eye, staged, in_sem, out_sem = refs[12], refs[13:18], refs[18], refs[19]
    t = pl.program_id(0)
    cols = comm.shape[2]
    step = eye.shape[0]
    loads = [pltpu.make_async_copy(a, b, in_sem.at[i]) for i, (a, b) in enumerate(zip(smalls, staged))]
    stores = [pltpu.make_async_copy(a, b, out_sem.at[i]) for i, (a, b) in enumerate(zip(staged, copied))]

    @pl.when(t == 0)
    def _():
        for copy in loads:
            copy.start()
        row = lax.broadcasted_iota(jnp.int32, eye.shape, 0)
        col = lax.broadcasted_iota(jnp.int32, eye.shape, 1)
        eye[...] = jnp.where(row == col, 1.0, 0.0).astype(bf16)

    @pl.when(t == 2)
    def _():
        for copy in loads:
            copy.wait()
        for copy in stores:
            copy.start()

    for z in range(4):
        for u in range(2):
            slots = [4 * (4 * u + i) + z for i in range(4)]
            found = [comm[0, TILE * n : TILE * (n + 1), :].astype(f32) for n in slots]
            row = 32 * z + 16 * u
            for kk in range(4):
                rows = jnp.concatenate([v[4 * kk : 4 * kk + 4] for v in found], axis=0)
                weights[row : row + 16, kk * cols : (kk + 1) * cols] = rows.astype(bf16)
    for i in range(4 * cols // step):
        block = weights[:, i * step : (i + 1) * step]
        if i % 2 == 0:
            turned = lax.dot_general(
                eye[...], block, (((1,), (1,)), ((), ())), preferred_element_type=f32
            )
        else:
            turned = block.astype(f32).T
        transposed[i * step : (i + 1) * step, :] = turned.astype(bf16)

    @pl.when(t == pl.num_programs(0) - 1)
    def _():
        for copy in stores:
            copy.wait()


def assemble(comm, smalls):
    rows = comm.shape[1] // 4
    d = comm.shape[0] * comm.shape[2] * 4
    cols = d // 4 // CHUNKS
    per = CHUNKS // GROUPS
    anywhere = pl.BlockSpec(memory_space=pl.ANY)
    return pl.pallas_call(
        assemble_kernel,
        grid=(CHUNKS,),
        out_shape=(
            jax.ShapeDtypeStruct((rows, d), bf16),
            jax.ShapeDtypeStruct((d, rows), bf16),
        )
        + tuple(jax.ShapeDtypeStruct(s.shape, s.dtype) for s in smalls),
        in_specs=[pl.BlockSpec((1, rows * 4, cols), lambda k: (k // per, 0, lax.rem(k, per)))]
        + [anywhere] * 5,
        out_specs=(
            pl.BlockSpec((rows, 4 * cols), lambda k: (0, k)),
            pl.BlockSpec((4 * cols, rows), lambda k: (k, 0)),
        )
        + (anywhere,) * 5,
        scratch_shapes=[pltpu.VMEM((256, 256), bf16)]
        + [pltpu.VMEM(s.shape, s.dtype) for s in smalls]
        + [pltpu.SemaphoreType.DMA((5,)), pltpu.SemaphoreType.DMA((5,))],
        compiler_params=pltpu.CompilerParams(
            vmem_limit_bytes=60 * 1024 * 1024,
            dimension_semantics=("arbitrary",),
        ),
        name="assemble",
    )(comm, *smalls)


def fused_on_device(
    grad_values, grad_scales, master, first_moment, first_scale, second_moment, second_scale
):
    def flat(array):
        return array.reshape(array.shape[-2:])

    comm, *smalls = exchange(
        flat(grad_values),
        flat(grad_scales).T,
        flat(master),
        flat(first_moment),
        flat(first_scale),
        flat(second_moment),
        flat(second_scale),
    )
    weights, transposed, *smalls = assemble(comm, smalls)
    return tuple(array[None] for array in (*smalls, weights, transposed))


def expand(values, scales):
    shape = values.shape
    blocks = values.astype(f32).reshape(shape[:-1] + (shape[-1] // BLOCK, BLOCK))
    return (blocks * scales.astype(f32)[..., None]).reshape(shape)


def quantize_blocks(values, signed):
    shape = values.shape
    blocks = values.reshape(shape[:-1] + (shape[-1] // BLOCK, BLOCK))
    if signed:
        peak = jnp.max(jnp.abs(blocks), axis=-1) + scale_eps
    else:
        peak = jnp.max(blocks, axis=-1) + scale_eps
    coded = (blocks / peak[..., None]).astype(bf16).reshape(shape)
    return (coded, peak)


def adam_step(gradient, master, first_moment, first_scale, second_moment, second_scale):
    first = beta_one * expand(first_moment, first_scale) + (1.0 - beta_one) * gradient
    second = beta_two * expand(second_moment, second_scale) + (1.0 - beta_two) * gradient * gradient
    direction = first / corr_one / (jnp.sqrt(second / corr_two) + adam_eps)
    updated = master - rate * direction
    first_coded, first_peak = quantize_blocks(first, True)
    second_coded, second_peak = quantize_blocks(second, False)
    return (updated, first_coded, first_peak, second_coded, second_peak, updated.astype(bf16))


def on_device(
    grad_values, grad_scales, master, first_moment, first_scale, second_moment, second_scale
):
    arrived, arrived_scales = (
        lax.all_to_all(grad_values, "group", split_axis=3, concat_axis=1, tiled=True),
        lax.all_to_all(grad_scales, "group", split_axis=3, concat_axis=1, tiled=True),
    )
    partial_sum = jnp.sum(expand(arrived, arrived_scales), axis=1)
    partial_sum = partial_sum.reshape(master.shape)
    gradient = lax.psum(partial_sum, "node")
    result = adam_step(gradient, master, first_moment, first_scale, second_moment, second_scale)
    updated, first_coded, first_peak, second_coded, second_peak, low_weights = result
    weights = lax.all_gather(low_weights, "group", axis=1, tiled=True)
    transposed = jnp.swapaxes(weights, 1, 2)
    return (updated, first_coded, first_peak, second_coded, second_peak, weights, transposed)


def solution(mesh):
    placed = (
        P("node", "group", "fsdp", None, None),
        P("node", "group", "fsdp", None, None),
        P("fsdp", "group", None),
        P("fsdp", "group", None),
        P("fsdp", "group", None),
        P("fsdp", "group", None),
        P("fsdp", "group", None),
    )
    fused = mesh.shape["node"] == 1 and mesh.shape["group"] == 32
    return jax.shard_map(
        fused_on_device if fused else on_device,
        mesh=mesh,
        in_specs=placed,
        out_specs=(
            P("fsdp", "group", None),
            P("fsdp", "group", None),
            P("fsdp", "group", None),
            P("fsdp", "group", None),
            P("fsdp", "group", None),
            P("fsdp", None, None),
            P("fsdp", None, None),
        ),
        check_vma=False,
    )
```

```python
import functools

import jax
import jax.numpy as jnp
from jax import lax
from jax.experimental import pallas as pl
from jax.experimental.pallas import tpu as pltpu
from jax.sharding import PartitionSpec as P

BLOCK = 128
CHUNKS = 8
GROUPS = 8
TILE = 16

beta_one = 0.9
beta_two = 0.95
rate = 0.02
adam_eps = 1e-08
scale_eps = 1e-06
corr_one = 1.0 - 0.9**10
corr_two = 1.0 - 0.95**10

f32 = jnp.float32
bf16 = jnp.bfloat16


def exchange_kernel(
    grad, gscale, master_in, fm_in, fs_in, sm_in, ss_in,
    comm, master_out, first_out, fs_out, second_out, ss_out,
    own, sib, sc_own, sc_sib, sh_own, sh_sib, part, rx1, rx2, acc, rx3, gfull, fbase, sbase, slotf, slot, held,
    master, fm, fs, sm, ss, new_master, new_first, new_fs, new_second, new_ss,
    in_sem, out_sem, own_sem, sc_sem, sib_sem, p1_sem, p2_sem, z_sem, g_sem,
    az_sem, ax_sem, ay_sem, fx_sem, fy_sem, as_sem, loc_sem,
):
    w = grad.shape[1] // 2 // CHUNKS
    nb = w // BLOCK
    me = lax.axis_index("group")
    c = lax.rem(me, 2)
    x = lax.rem(me // 2, 2)
    y = lax.rem(me // 4, 2)
    z = me // 8

    def index(zz, yy, xx, cc):
        return zz * 8 + yy * 4 + xx * 2 + cc

    sibling = index(z, y, x, 1 - c)
    xn = index(z, y, 1 - x, c)
    yn = index(z, 1 - y, x, c)
    z_up = [lax.rem(z + d, 4) for d in range(4)]
    z_from = [lax.rem(z + 4 - d, 4) for d in range(4)]
    zn = [index(z_up[d], y, x, c) for d in range(4)]

    def remote(src, dst, sems, at, to):
        return pltpu.make_async_remote_copy(
            src_ref=src,
            dst_ref=dst,
            send_sem=sems.at[(0,) + at],
            recv_sem=sems.at[(1,) + at],
            device_id={"group": to},
            device_id_type=pl.DeviceIdType.MESH,
        )

    sent = []

    def send(*args):
        copy = remote(*args)
        copy.start()
        sent.append(copy)
        return copy

    def local(src, dst, sem):
        copy = pltpu.make_async_copy(src, dst, sem)
        copy.start()
        return copy

    def columns(k, h):
        return k * 2 * w + h * w

    scale_own = local(gscale, sc_own, in_sem.at[5])
    own_copies = []
    for k in range(CHUNKS):
        here = pl.multiple_of(columns(k, c), BLOCK)
        own_copies.append(local(grad.at[:, pl.ds(here, w)], own.at[k], own_sem.at[k]))

    barrier = pltpu.get_barrier_semaphore()
    partners = [sibling, xn, yn] + zn[1:]
    for to in partners:
        pl.semaphore_signal(
            barrier, inc=1, device_id={"group": to}, device_id_type=pl.DeviceIdType.MESH
        )
    pl.semaphore_wait(barrier, len(partners))

    scale_copy = send(gscale, sc_sib, sc_sem, (0,), sibling)
    sib_copies = []
    for k in range(CHUNKS):
        there = pl.multiple_of(columns(k, 1 - c), BLOCK)
        sib_copies.append(send(grad.at[:, pl.ds(there, w)], sib.at[k], sib_sem, (k,), sibling))
    fetched = [
        local(src, dst, in_sem.at[i])
        for i, (src, dst) in enumerate(
            ((fm_in, fm), (fs_in, fs), (sm_in, sm), (ss_in, ss), (master_in, master))
        )
    ]

    def half_scales(ref, out):
        values = ref[...].astype(f32).T
        for k in range(CHUNKS):
            j = 2 * k * nb
            out[:, k * nb : (k + 1) * nb] = jnp.where(
                c == 0, values[:, j : j + nb], values[:, j + nb : j + 2 * nb]
            )

    scale_own.wait()
    half_scales(sc_own, sh_own)
    scale_copy.wait_recv()
    half_scales(sc_sib, sh_sib)

    def order(k):
        return (x, y, xn, yn) if k % 2 == 0 else (y, x, yn, xn)

    p1, p2 = {}, {}

    def core_sum(k):
        own_copies[k].wait()
        sib_copies[k].wait_recv()

        def body(i, carry):
            rows = pl.ds(pl.multiple_of(i * 16, 16), 16)
            so, sb = sh_own[rows, :], sh_sib[rows, :]
            zz, yy = i // 2, lax.rem(i, 2)
            for b in range(nb):
                j = k * nb + b
                cols = pl.ds(b * BLOCK, BLOCK)
                v = own[k, rows, cols].astype(f32) * so[:, j : j + 1]
                v += sib[k, rows, cols].astype(f32) * sb[:, j : j + 1]
                for xx in range(2):
                    one, two = (xx, yy) if k % 2 == 0 else (yy, xx)
                    part[k, one, two, zz, :, cols] = v[8 * xx : 8 * xx + 8]
            return carry

        lax.fori_loop(0, 8, body, 0)
        a, _, an, _ = order(k)
        p1[k] = send(part.at[k, 1 - a], rx1.at[k], p1_sem, (k,), an)

    def base(k):
        for b in range(2 * nb):
            j = 2 * k * nb + b
            cols = pl.ds(j * BLOCK, BLOCK)
            fbase[:, cols] = beta_one * (fm[:, cols].astype(f32) * fs[:, j : j + 1])
            sbase[:, cols] = beta_two * (sm[:, cols].astype(f32) * ss[:, j : j + 1])

    def first_axis(k):
        a, b, _, bn = order(k)
        p1[k].wait_recv()
        for zz in range(4):
            part[k, a, 1 - b, zz] = part[k, a, 1 - b, zz] + rx1[k, 1 - b, zz]
        p2[k] = send(part.at[k, a, 1 - b], rx2.at[k], p2_sem, (k,), bn)

    def second_axis(k):
        a, b, _, _ = order(k)
        p2[k].wait_recv()
        for zz in range(4):
            acc[k, zz] = part[k, a, b, zz] + rx1[k, b, zz] + rx2[k, zz]
        for d in range(1, 4):
            send(acc.at[k, z_up[d]], rx3.at[k, d], z_sem, (k, d), zn[d])

    def along_z(k):
        total = acc[k, z]
        for d in range(1, 4):
            remote(acc.at[k, z_up[d]], rx3.at[k, d], z_sem, (k, d), zn[d]).wait_recv()
            total = total + rx3[k, d]
        gfull[c, k] = total
        send(gfull.at[c, k], gfull.at[c, k], g_sem, (k,), sibling)

    def adam(k):
        remote(gfull.at[1 - c, k], gfull.at[1 - c, k], g_sem, (k,), sibling).wait_recv()
        for h in range(2):
            cols = pl.ds(columns(k, h), w)
            v = gfull[h, k]
            g = jnp.where(c == 0, v[0:4], v[4:8])
            first = fbase[:, cols] + (1.0 - beta_one) * g
            second = sbase[:, cols] + (1.0 - beta_two) * g * g
            fbase[:, cols] = first
            sbase[:, cols] = second
            direction = first / corr_one / (jnp.sqrt(second / corr_two) + adam_eps)
            updated = master[:, cols] - rate * direction
            new_master[:, cols] = updated
            for q in range(2):
                r = 4 * (2 * h + q)
                slotf[r : r + 4, k * (w // 2) : (k + 1) * (w // 2)] = updated[
                    :, q * (w // 2) : (q + 1) * (w // 2)
                ]

    def quantize(k):
        for b in range(2 * nb):
            j = 2 * k * nb + b
            cols = pl.ds(j * BLOCK, BLOCK)
            first, second = fbase[:, cols], sbase[:, cols]
            peak = jnp.max(jnp.abs(first), axis=1, keepdims=True) + scale_eps
            new_fs[:, j : j + 1] = peak
            new_first[:, cols] = (first / peak).astype(bf16)
            peak = jnp.max(second, axis=1, keepdims=True) + scale_eps
            new_ss[:, j : j + 1] = peak
            new_second[:, cols] = (second / peak).astype(bf16)

    per = CHUNKS // GROUPS
    wide = per * (w // 2)
    nearly_half = [(wide // BLOCK + e % 2) // 2 * BLOCK for e in range(GROUPS)]
    placed = []

    def place(e, yy, xx, cc, zz=None, lo=0, width=wide):
        row = pl.multiple_of(index(0, yy, xx, cc) * 4 * TILE, TILE)
        count = 4 * TILE
        if zz is not None:
            row, count = pl.multiple_of(row + zz * TILE, TILE), TILE
        return held.at[e, pl.ds(row, count), pl.ds(lo, width)]

    def gather_own(e):
        cols = pl.ds(e * wide, wide)
        slot[:, cols] = slotf[:, cols].astype(bf16)
        src, dst = slot.at[:, cols], place(e, y, x, c, z)
        for d in range(1, 4):
            send(src, dst, az_sem, (e, d), zn[d])
        placed.append(local(src, dst, loc_sem.at[e]))

    def gather_z(e):
        placed[e].wait()
        for d in range(1, 4):
            ref = place(e, y, x, c, z_from[d])
            remote(ref, ref, az_sem, (e, d), zn[d]).wait_recv()
        ref = place(e, y, x, c)
        send(ref, ref, ax_sem, (e,), xn)
        send(ref, ref, ay_sem, (e,), yn)
        send(ref, ref, as_sem, (e, 0), sibling)

    def gather_xy(e):
        ref = place(e, y, 1 - x, c)
        remote(ref, ref, ax_sem, (e,), xn).wait_recv()
        right = place(e, y, 1 - x, c, None, nearly_half[e], wide - nearly_half[e])
        send(right, right, fy_sem, (e,), yn)
        other = place(e, 1 - y, x, c)
        remote(other, other, ay_sem, (e,), yn).wait_recv()
        left = place(e, 1 - y, x, c, None, 0, nearly_half[e])
        send(left, left, fx_sem, (e,), xn)
        send(ref, ref, as_sem, (e, 1), sibling)
        send(other, other, as_sem, (e, 2), sibling)

    def gather_far(e):
        left = place(e, 1 - y, 1 - x, c, None, 0, nearly_half[e])
        right = place(e, 1 - y, 1 - x, c, None, nearly_half[e], wide - nearly_half[e])
        remote(left, left, fx_sem, (e,), xn).wait_recv()
        remote(right, right, fy_sem, (e,), yn).wait_recv()
        ref = place(e, 1 - y, 1 - x, c)
        send(ref, ref, as_sem, (e, 3), sibling)

    def gather_end(e):
        for q in range(4):
            yy = 1 - y if q >= 2 else y
            xx = 1 - x if q % 2 == 1 else x
            ref = place(e, yy, xx, 1 - c)
            remote(ref, ref, as_sem, (e, q), sibling).wait_recv()
        return local(held.at[e], comm.at[e], loc_sem.at[e])

    def chunks(e):
        return range(e * per, (e + 1) * per)

    def each(f, e):
        if 0 <= e < GROUPS:
            for k in chunks(e):
                f(k)

    def group(f, e):
        if 0 <= e < GROUPS:
            f(e)

    ahead = 4
    for e in range(ahead):
        each(core_sum, e)
    for copy in fetched:
        copy.wait()
    for e in range(ahead):
        each(base, e)
    for t in range(GROUPS + 7):
        each(first_axis, t)
        each(core_sum, t + ahead)
        each(base, t + ahead)
        each(second_axis, t - 2)
        each(along_z, t - 3)
        group(gather_far, t - 6)
        group(gather_xy, t - 5)
        each(adam, t - 3)
        group(gather_own, t - 3)
        group(gather_z, t - 4)
        each(quantize, t - 5)
    stored = [
        local(src, dst, out_sem.at[i])
        for i, (src, dst) in enumerate(
            (
                (new_master, master_out),
                (new_first, first_out),
                (new_fs, fs_out),
                (new_second, second_out),
                (new_ss, ss_out),
            )
        )
    ]
    for e in range(GROUPS):
        stored.append(gather_end(e))
    for copy in sent:
        copy.wait_send()
    for copy in stored:
        copy.wait()


def exchange(grad, gscale, master, fm, fs, sm, ss):
    rows, d = grad.shape
    own_rows = master.shape[0]
    w = d // 2 // CHUNKS
    K, G = CHUNKS, GROUPS
    anywhere = pl.BlockSpec(memory_space=pl.ANY)
    dma = pltpu.SemaphoreType.DMA
    smalls = (master, fm, fs, sm, ss)
    return pl.pallas_call(
        exchange_kernel,
        out_shape=(jax.ShapeDtypeStruct((G, rows * 4, d // 4 // G), bf16),)
        + tuple(jax.ShapeDtypeStruct(s.shape, s.dtype) for s in smalls),
        in_specs=[anywhere] * 7,
        out_specs=(anywhere,) * 6,
        scratch_shapes=[
            pltpu.VMEM((K, rows, w), bf16),
            pltpu.VMEM((K, rows, w), bf16),
            pltpu.VMEM(gscale.shape, bf16),
            pltpu.VMEM(gscale.shape, bf16),
            pltpu.VMEM((rows, gscale.shape[0] // 2), f32),
            pltpu.VMEM((rows, gscale.shape[0] // 2), f32),
            pltpu.VMEM((K, 2, 2, 4, 8, w), f32),
            pltpu.VMEM((K, 2, 4, 8, w), f32),
            pltpu.VMEM((K, 4, 8, w), f32),
            pltpu.VMEM((K, 4, 8, w), f32),
            pltpu.VMEM((K, 4, 8, w), f32),
            pltpu.VMEM((2, K, 8, w), f32),
            pltpu.VMEM((own_rows, d), f32),
            pltpu.VMEM((own_rows, d), f32),
            pltpu.VMEM((TILE, d // 4), f32),
            pltpu.VMEM((TILE, d // 4), bf16),
            pltpu.VMEM((G, rows * 4, d // 4 // G), bf16),
        ]
        + [pltpu.VMEM(s.shape, s.dtype) for s in smalls + smalls]
        + [
            dma((6,)),
            dma((5,)),
            dma((K,)),
            dma((2, 1)),
            dma((2, K)),
            dma((2, K)),
            dma((2, K)),
            dma((2, K, 4)),
            dma((2, K)),
            dma((2, G, 4)),
            dma((2, G)),
            dma((2, G)),
            dma((2, G)),
            dma((2, G)),
            dma((2, G, 4)),
            dma((G,)),
        ],
        compiler_params=pltpu.CompilerParams(
            collective_id=0, has_side_effects=True, vmem_limit_bytes=60 * 1024 * 1024
        ),
        cost_estimate=pl.CostEstimate(
            flops=8 * rows * d, bytes_accessed=8 * rows * d, transcendentals=own_rows * d
        ),
        name="exchange",
    )(grad, gscale, master, fm, fs, sm, ss)


def assemble_kernel(comm, *refs):
    smalls, (weights, transposed), copied = refs[:5], refs[5:7], refs[7:12]
    eye, staged, in_sem, out_sem = refs[12], refs[13:18], refs[18], refs[19]
    t = pl.program_id(0)
    cols = comm.shape[2]
    step = eye.shape[0]
    loads = [pltpu.make_async_copy(a, b, in_sem.at[i]) for i, (a, b) in enumerate(zip(smalls, staged))]
    stores = [pltpu.make_async_copy(a, b, out_sem.at[i]) for i, (a, b) in enumerate(zip(staged, copied))]

    @pl.when(t == 0)
    def _():
        for copy in loads:
            copy.start()
        row = lax.broadcasted_iota(jnp.int32, eye.shape, 0)
        col = lax.broadcasted_iota(jnp.int32, eye.shape, 1)
        eye[...] = jnp.where(row == col, 1.0, 0.0).astype(bf16)

    @pl.when(t == 2)
    def _():
        for copy in loads:
            copy.wait()
        for copy in stores:
            copy.start()

    for z in range(4):
        for u in range(2):
            slots = [4 * (4 * u + i) + z for i in range(4)]
            found = [comm[0, TILE * n : TILE * (n + 1), :].astype(f32) for n in slots]
            row = 32 * z + 16 * u
            for kk in range(4):
                rows = jnp.concatenate([v[4 * kk : 4 * kk + 4] for v in found], axis=0)
                weights[row : row + 16, kk * cols : (kk + 1) * cols] = rows.astype(bf16)
    for i in range(4 * cols // step):
        block = weights[:, i * step : (i + 1) * step]
        if i % 2 == 0:
            turned = lax.dot_general(
                eye[...], block, (((1,), (1,)), ((), ())), preferred_element_type=f32
            )
        else:
            turned = block.T
        transposed[i * step : (i + 1) * step, :] = turned.astype(bf16)

    @pl.when(t == pl.num_programs(0) - 1)
    def _():
        for copy in stores:
            copy.wait()


def assemble(comm, smalls):
    rows = comm.shape[1] // 4
    d = comm.shape[0] * comm.shape[2] * 4
    cols = d // 4 // CHUNKS
    per = CHUNKS // GROUPS
    anywhere = pl.BlockSpec(memory_space=pl.ANY)
    return pl.pallas_call(
        assemble_kernel,
        grid=(CHUNKS,),
        out_shape=(
            jax.ShapeDtypeStruct((rows, d), bf16),
            jax.ShapeDtypeStruct((d, rows), bf16),
        )
        + tuple(jax.ShapeDtypeStruct(s.shape, s.dtype) for s in smalls),
        in_specs=[pl.BlockSpec((1, rows * 4, cols), lambda k: (k // per, 0, lax.rem(k, per)))]
        + [anywhere] * 5,
        out_specs=(
            pl.BlockSpec((rows, 4 * cols), lambda k: (0, k)),
            pl.BlockSpec((4 * cols, rows), lambda k: (k, 0)),
        )
        + (anywhere,) * 5,
        scratch_shapes=[pltpu.VMEM((256, 256), bf16)]
        + [pltpu.VMEM(s.shape, s.dtype) for s in smalls]
        + [pltpu.SemaphoreType.DMA((5,)), pltpu.SemaphoreType.DMA((5,))],
        compiler_params=pltpu.CompilerParams(
            vmem_limit_bytes=60 * 1024 * 1024,
            dimension_semantics=("arbitrary",),
        ),
        name="assemble",
    )(comm, *smalls)


def fused_on_device(
    grad_values, grad_scales, master, first_moment, first_scale, second_moment, second_scale
):
    def flat(array):
        return array.reshape(array.shape[-2:])

    comm, *smalls = exchange(
        flat(grad_values),
        flat(grad_scales).T,
        flat(master),
        flat(first_moment),
        flat(first_scale),
        flat(second_moment),
        flat(second_scale),
    )
    weights, transposed, *smalls = assemble(comm, smalls)
    return tuple(array[None] for array in (*smalls, weights, transposed))


def expand(values, scales):
    shape = values.shape
    blocks = values.astype(f32).reshape(shape[:-1] + (shape[-1] // BLOCK, BLOCK))
    return (blocks * scales.astype(f32)[..., None]).reshape(shape)


def quantize_blocks(values, signed):
    shape = values.shape
    blocks = values.reshape(shape[:-1] + (shape[-1] // BLOCK, BLOCK))
    if signed:
        peak = jnp.max(jnp.abs(blocks), axis=-1) + scale_eps
    else:
        peak = jnp.max(blocks, axis=-1) + scale_eps
    coded = (blocks / peak[..., None]).astype(bf16).reshape(shape)
    return (coded, peak)


def adam_step(gradient, master, first_moment, first_scale, second_moment, second_scale):
    first = beta_one * expand(first_moment, first_scale) + (1.0 - beta_one) * gradient
    second = beta_two * expand(second_moment, second_scale) + (1.0 - beta_two) * gradient * gradient
    direction = first / corr_one / (jnp.sqrt(second / corr_two) + adam_eps)
    updated = master - rate * direction
    first_coded, first_peak = quantize_blocks(first, True)
    second_coded, second_peak = quantize_blocks(second, False)
    return (updated, first_coded, first_peak, second_coded, second_peak, updated.astype(bf16))


def on_device(
    grad_values, grad_scales, master, first_moment, first_scale, second_moment, second_scale
):
    arrived, arrived_scales = (
        lax.all_to_all(grad_values, "group", split_axis=3, concat_axis=1, tiled=True),
        lax.all_to_all(grad_scales, "group", split_axis=3, concat_axis=1, tiled=True),
    )
    partial_sum = jnp.sum(expand(arrived, arrived_scales), axis=1)
    partial_sum = partial_sum.reshape(master.shape)
    gradient = lax.psum(partial_sum, "node")
    result = adam_step(gradient, master, first_moment, first_scale, second_moment, second_scale)
    updated, first_coded, first_peak, second_coded, second_peak, low_weights = result
    weights = lax.all_gather(low_weights, "group", axis=1, tiled=True)
    transposed = jnp.swapaxes(weights, 1, 2)
    return (updated, first_coded, first_peak, second_coded, second_peak, weights, transposed)


def solution(mesh):
    placed = (
        P("node", "group", "fsdp", None, None),
        P("node", "group", "fsdp", None, None),
        P("fsdp", "group", None),
        P("fsdp", "group", None),
        P("fsdp", "group", None),
        P("fsdp", "group", None),
        P("fsdp", "group", None),
    )
    fused = mesh.shape["node"] == 1 and mesh.shape["group"] == 32
    return jax.shard_map(
        fused_on_device if fused else on_device,
        mesh=mesh,
        in_specs=placed,
        out_specs=(
            P("fsdp", "group", None),
            P("fsdp", "group", None),
            P("fsdp", "group", None),
            P("fsdp", "group", None),
            P("fsdp", "group", None),
            P("fsdp", None, None),
            P("fsdp", None, None),
        ),
        check_vma=False,
    )
```

```python
import functools

import jax
import jax.numpy as jnp
from jax import lax
from jax.experimental import pallas as pl
from jax.experimental.pallas import tpu as pltpu
from jax.sharding import PartitionSpec as P

BLOCK = 128
CHUNKS = 8
PARTS = (0, 3, 5, 7, 8)
GROUPS = len(PARTS) - 1
TILE = 16

beta_one = 0.9
beta_two = 0.95
rate = 0.02
adam_eps = 1e-08
scale_eps = 1e-06
corr_one = 1.0 - 0.9**10
corr_two = 1.0 - 0.95**10

f32 = jnp.float32
bf16 = jnp.bfloat16


def exchange_kernel(
    grad, gscale, master_in, fm_in, fs_in, sm_in, ss_in,
    comm, master_out, first_out, fs_out, second_out, ss_out,
    own, sib, sc_own, sc_sib, sh_own, sh_sib, part, rx1, rx2, acc, rx3, gfull, fbase, sbase, slotf, slot, held,
    master, fm, fs, sm, ss, new_master, new_first, new_fs, new_second, new_ss,
    in_sem, out_sem, own_sem, sc_sem, sib_sem, p1_sem, p2_sem, z_sem, g_sem,
    az_sem, ax_sem, ay_sem, fx_sem, fy_sem, as_sem, loc_sem,
):
    w = grad.shape[1] // 2 // CHUNKS
    nb = w // BLOCK
    me = lax.axis_index("group")
    c = lax.rem(me, 2)
    x = lax.rem(me // 2, 2)
    y = lax.rem(me // 4, 2)
    z = me // 8

    def index(zz, yy, xx, cc):
        return zz * 8 + yy * 4 + xx * 2 + cc

    sibling = index(z, y, x, 1 - c)
    xn = index(z, y, 1 - x, c)
    yn = index(z, 1 - y, x, c)
    z_up = [lax.rem(z + d, 4) for d in range(4)]
    z_from = [lax.rem(z + 4 - d, 4) for d in range(4)]
    zn = [index(z_up[d], y, x, c) for d in range(4)]

    def remote(src, dst, sems, at, to):
        return pltpu.make_async_remote_copy(
            src_ref=src,
            dst_ref=dst,
            send_sem=sems.at[(0,) + at],
            recv_sem=sems.at[(1,) + at],
            device_id={"group": to},
            device_id_type=pl.DeviceIdType.MESH,
        )

    sent = []

    def send(*args):
        copy = remote(*args)
        copy.start()
        sent.append(copy)
        return copy

    def local(src, dst, sem):
        copy = pltpu.make_async_copy(src, dst, sem)
        copy.start()
        return copy

    def columns(k, h):
        return k * 2 * w + h * w

    scale_own = local(gscale, sc_own, in_sem.at[5])
    own_copies = []
    for k in range(CHUNKS):
        here = pl.multiple_of(columns(k, c), BLOCK)
        own_copies.append(local(grad.at[:, pl.ds(here, w)], own.at[k], own_sem.at[k]))

    barrier = pltpu.get_barrier_semaphore()
    partners = [sibling, xn, yn] + zn[1:]
    for to in partners:
        pl.semaphore_signal(
            barrier, inc=1, device_id={"group": to}, device_id_type=pl.DeviceIdType.MESH
        )
    pl.semaphore_wait(barrier, len(partners))

    scale_copy = send(gscale, sc_sib, sc_sem, (0,), sibling)
    sib_copies = []
    for k in range(CHUNKS):
        there = pl.multiple_of(columns(k, 1 - c), BLOCK)
        sib_copies.append(send(grad.at[:, pl.ds(there, w)], sib.at[k], sib_sem, (k,), sibling))
    fetched = [
        local(src, dst, in_sem.at[i])
        for i, (src, dst) in enumerate(
            ((fm_in, fm), (fs_in, fs), (sm_in, sm), (ss_in, ss), (master_in, master))
        )
    ]

    def half_scales(ref, out):
        values = ref[...].astype(f32).T
        for k in range(CHUNKS):
            j = 2 * k * nb
            out[:, k * nb : (k + 1) * nb] = jnp.where(
                c == 0, values[:, j : j + nb], values[:, j + nb : j + 2 * nb]
            )

    scale_own.wait()
    half_scales(sc_own, sh_own)
    scale_copy.wait_recv()
    half_scales(sc_sib, sh_sib)

    def order(k):
        return (x, y, xn, yn) if k % 2 == 0 else (y, x, yn, xn)

    p1, p2 = {}, {}

    def core_sum(k):
        own_copies[k].wait()
        sib_copies[k].wait_recv()

        def body(i, carry):
            rows = pl.ds(pl.multiple_of(i * 16, 16), 16)
            so, sb = sh_own[rows, :], sh_sib[rows, :]
            zz, yy = i // 2, lax.rem(i, 2)
            for b in range(nb):
                j = k * nb + b
                cols = pl.ds(b * BLOCK, BLOCK)
                v = own[k, rows, cols].astype(f32) * so[:, j : j + 1]
                v += sib[k, rows, cols].astype(f32) * sb[:, j : j + 1]
                for xx in range(2):
                    one, two = (xx, yy) if k % 2 == 0 else (yy, xx)
                    part[k, one, two, zz, :, cols] = v[8 * xx : 8 * xx + 8]
            return carry

        lax.fori_loop(0, 8, body, 0)
        a, _, an, _ = order(k)
        p1[k] = send(part.at[k, 1 - a], rx1.at[k], p1_sem, (k,), an)

    def base(k):
        for b in range(2 * nb):
            j = 2 * k * nb + b
            cols = pl.ds(j * BLOCK, BLOCK)
            fbase[:, cols] = beta_one * (fm[:, cols].astype(f32) * fs[:, j : j + 1])
            sbase[:, cols] = beta_two * (sm[:, cols].astype(f32) * ss[:, j : j + 1])

    def first_axis(k):
        a, b, _, bn = order(k)
        p1[k].wait_recv()
        for zz in range(4):
            part[k, a, 1 - b, zz] = part[k, a, 1 - b, zz] + rx1[k, 1 - b, zz]
        p2[k] = send(part.at[k, a, 1 - b], rx2.at[k], p2_sem, (k,), bn)

    def second_axis(k):
        a, b, _, _ = order(k)
        p2[k].wait_recv()
        for zz in range(4):
            acc[k, zz] = part[k, a, b, zz] + rx1[k, b, zz] + rx2[k, zz]
        for d in range(1, 4):
            send(acc.at[k, z_up[d]], rx3.at[k, d], z_sem, (k, d), zn[d])

    def along_z(k):
        total = acc[k, z]
        for d in range(1, 4):
            remote(acc.at[k, z_up[d]], rx3.at[k, d], z_sem, (k, d), zn[d]).wait_recv()
            total = total + rx3[k, d]
        gfull[c, k] = total
        send(gfull.at[c, k], gfull.at[c, k], g_sem, (k,), sibling)

    def adam(k):
        remote(gfull.at[1 - c, k], gfull.at[1 - c, k], g_sem, (k,), sibling).wait_recv()
        for h in range(2):
            cols = pl.ds(columns(k, h), w)
            v = gfull[h, k]
            g = jnp.where(c == 0, v[0:4], v[4:8])
            first = fbase[:, cols] + (1.0 - beta_one) * g
            second = sbase[:, cols] + (1.0 - beta_two) * g * g
            fbase[:, cols] = first
            sbase[:, cols] = second
            direction = first / corr_one / (jnp.sqrt(second / corr_two) + adam_eps)
            updated = master[:, cols] - rate * direction
            new_master[:, cols] = updated
            for q in range(2):
                r = 4 * (2 * h + q)
                slotf[r : r + 4, k * (w // 2) : (k + 1) * (w // 2)] = updated[
                    :, q * (w // 2) : (q + 1) * (w // 2)
                ]

    def quantize(k):
        for b in range(2 * nb):
            j = 2 * k * nb + b
            cols = pl.ds(j * BLOCK, BLOCK)
            first, second = fbase[:, cols], sbase[:, cols]
            peak = jnp.max(jnp.abs(first), axis=1, keepdims=True) + scale_eps
            new_fs[:, j : j + 1] = peak
            new_first[:, cols] = (first / peak).astype(bf16)
            peak = jnp.max(second, axis=1, keepdims=True) + scale_eps
            new_ss[:, j : j + 1] = peak
            new_second[:, cols] = (second / peak).astype(bf16)

    wide = w // 2
    placed = []

    def place(e, yy, xx, cc, first=0, count=4):
        row = pl.multiple_of((index(0, yy, xx, cc) * 4 + first) * TILE, TILE)
        return held.at[PARTS[e] : PARTS[e + 1], pl.ds(row, count * TILE)]

    def gather_own(e):
        for k in chunks(e):
            slot[k] = slotf[:, k * wide : (k + 1) * wide].astype(bf16)
        src, dst = slot.at[PARTS[e] : PARTS[e + 1]], place(e, y, x, c, z, 1)
        for d in range(1, 4):
            send(src, dst, az_sem, (e, d), zn[d])
        placed.append(local(src, dst, loc_sem.at[e]))

    def gather_z(e):
        placed[e].wait()
        for d in range(1, 4):
            ref = place(e, y, x, c, z_from[d], 1)
            remote(ref, ref, az_sem, (e, d), zn[d]).wait_recv()
        ref = place(e, y, x, c)
        send(ref, ref, ax_sem, (e,), xn)
        send(ref, ref, ay_sem, (e,), yn)
        send(ref, ref, as_sem, (e, 0), sibling)

    def gather_xy(e):
        ref = place(e, y, 1 - x, c)
        remote(ref, ref, ax_sem, (e,), xn).wait_recv()
        right = place(e, y, 1 - x, c, 2, 2)
        send(right, right, fy_sem, (e,), yn)
        other = place(e, 1 - y, x, c)
        remote(other, other, ay_sem, (e,), yn).wait_recv()
        left = place(e, 1 - y, x, c, 0, 2)
        send(left, left, fx_sem, (e,), xn)
        send(ref, ref, as_sem, (e, 1), sibling)
        send(other, other, as_sem, (e, 2), sibling)

    def gather_far(e):
        left = place(e, 1 - y, 1 - x, c, 0, 2)
        right = place(e, 1 - y, 1 - x, c, 2, 2)
        remote(left, left, fx_sem, (e,), xn).wait_recv()
        remote(right, right, fy_sem, (e,), yn).wait_recv()
        ref = place(e, 1 - y, 1 - x, c)
        send(ref, ref, as_sem, (e, 3), sibling)

    def gather_end(e):
        for q in range(4):
            yy = 1 - y if q >= 2 else y
            xx = 1 - x if q % 2 == 1 else x
            ref = place(e, yy, xx, 1 - c)
            remote(ref, ref, as_sem, (e, q), sibling).wait_recv()
        part_of = slice(PARTS[e], PARTS[e + 1])
        return local(held.at[part_of], comm.at[part_of], loc_sem.at[e])

    def chunks(e):
        return range(PARTS[e], PARTS[e + 1])

    def each(f, e):
        if 0 <= e < GROUPS:
            for k in chunks(e):
                f(k)

    def group(f, e):
        if 0 <= e < GROUPS:
            f(e)

    ahead = 2
    for e in range(ahead):
        each(core_sum, e)
    for copy in fetched:
        copy.wait()
    for e in range(ahead):
        each(base, e)
    for t in range(GROUPS + 5):
        each(first_axis, t)
        each(core_sum, t + ahead)
        each(base, t + ahead)
        each(second_axis, t - 1)
        each(along_z, t - 2)
        each(adam, t - 2)
        group(gather_own, t - 2)
        group(gather_z, t - 3)
        group(gather_xy, t - 4)
        group(gather_far, t - 5)
        each(quantize, t - 3)
    stored = [
        local(src, dst, out_sem.at[i])
        for i, (src, dst) in enumerate(
            (
                (new_master, master_out),
                (new_first, first_out),
                (new_fs, fs_out),
                (new_second, second_out),
                (new_ss, ss_out),
            )
        )
    ]
    for e in range(GROUPS):
        stored.append(gather_end(e))
    for copy in sent:
        copy.wait_send()
    for copy in stored:
        copy.wait()


def exchange(grad, gscale, master, fm, fs, sm, ss):
    rows, d = grad.shape
    own_rows = master.shape[0]
    w = d // 2 // CHUNKS
    K, G = CHUNKS, GROUPS
    anywhere = pl.BlockSpec(memory_space=pl.ANY)
    dma = pltpu.SemaphoreType.DMA
    smalls = (master, fm, fs, sm, ss)
    return pl.pallas_call(
        exchange_kernel,
        out_shape=(jax.ShapeDtypeStruct((K, rows * 4, d // 4 // K), bf16),)
        + tuple(jax.ShapeDtypeStruct(s.shape, s.dtype) for s in smalls),
        in_specs=[anywhere] * 7,
        out_specs=(anywhere,) * 6,
        scratch_shapes=[
            pltpu.VMEM((K, rows, w), bf16),
            pltpu.VMEM((K, rows, w), bf16),
            pltpu.VMEM(gscale.shape, bf16),
            pltpu.VMEM(gscale.shape, bf16),
            pltpu.VMEM((rows, gscale.shape[0] // 2), f32),
            pltpu.VMEM((rows, gscale.shape[0] // 2), f32),
            pltpu.VMEM((K, 2, 2, 4, 8, w), f32),
            pltpu.VMEM((K, 2, 4, 8, w), f32),
            pltpu.VMEM((K, 4, 8, w), f32),
            pltpu.VMEM((K, 4, 8, w), f32),
            pltpu.VMEM((K, 4, 8, w), f32),
            pltpu.VMEM((2, K, 8, w), f32),
            pltpu.VMEM((own_rows, d), f32),
            pltpu.VMEM((own_rows, d), f32),
            pltpu.VMEM((TILE, d // 4), f32),
            pltpu.VMEM((K, TILE, d // 4 // K), bf16),
            pltpu.VMEM((K, rows * 4, d // 4 // K), bf16),
        ]
        + [pltpu.VMEM(s.shape, s.dtype) for s in smalls + smalls]
        + [
            dma((6,)),
            dma((5,)),
            dma((K,)),
            dma((2, 1)),
            dma((2, K)),
            dma((2, K)),
            dma((2, K)),
            dma((2, K, 4)),
            dma((2, K)),
            dma((2, G, 4)),
            dma((2, G)),
            dma((2, G)),
            dma((2, G)),
            dma((2, G)),
            dma((2, G, 4)),
            dma((G,)),
        ],
        compiler_params=pltpu.CompilerParams(
            collective_id=0, has_side_effects=True, vmem_limit_bytes=60 * 1024 * 1024
        ),
        cost_estimate=pl.CostEstimate(
            flops=8 * rows * d, bytes_accessed=8 * rows * d, transcendentals=own_rows * d
        ),
        name="exchange",
    )(grad, gscale, master, fm, fs, sm, ss)


def assemble_kernel(comm, *refs):
    smalls, (weights, transposed), copied = refs[:5], refs[5:7], refs[7:12]
    staged, in_sem, out_sem = refs[12:17], refs[17], refs[18]
    t = pl.program_id(0)
    cols = comm.shape[2]
    step = 2 * BLOCK
    loads = [pltpu.make_async_copy(a, b, in_sem.at[i]) for i, (a, b) in enumerate(zip(smalls, staged))]
    stores = [pltpu.make_async_copy(a, b, out_sem.at[i]) for i, (a, b) in enumerate(zip(staged, copied))]

    @pl.when(t == 0)
    def _():
        for copy in loads:
            copy.start()

    @pl.when(t == 2)
    def _():
        for copy in loads:
            copy.wait()
        for copy in stores:
            copy.start()

    for z in range(4):
        for u in range(2):
            slots = [4 * (4 * u + i) + z for i in range(4)]
            found = [comm[0, TILE * n : TILE * (n + 1), :].astype(f32) for n in slots]
            row = 32 * z + 16 * u
            for kk in range(4):
                rows = jnp.concatenate([v[4 * kk : 4 * kk + 4] for v in found], axis=0)
                weights[row : row + 16, kk * cols : (kk + 1) * cols] = rows.astype(bf16)
    for i in range(4 * cols // step):
        block = weights[:, i * step : (i + 1) * step]
        transposed[i * step : (i + 1) * step, :] = block.T

    @pl.when(t == pl.num_programs(0) - 1)
    def _():
        for copy in stores:
            copy.wait()


def assemble(comm, smalls):
    rows = comm.shape[1] // 4
    d = comm.shape[0] * comm.shape[2] * 4
    cols = d // 4 // CHUNKS
    anywhere = pl.BlockSpec(memory_space=pl.ANY)
    return pl.pallas_call(
        assemble_kernel,
        grid=(CHUNKS,),
        out_shape=(
            jax.ShapeDtypeStruct((rows, d), bf16),
            jax.ShapeDtypeStruct((d, rows), bf16),
        )
        + tuple(jax.ShapeDtypeStruct(s.shape, s.dtype) for s in smalls),
        in_specs=[pl.BlockSpec((1, rows * 4, cols), lambda k: (k, 0, 0))]
        + [anywhere] * 5,
        out_specs=(
            pl.BlockSpec((rows, 4 * cols), lambda k: (0, k)),
            pl.BlockSpec((4 * cols, rows), lambda k: (k, 0)),
        )
        + (anywhere,) * 5,
        scratch_shapes=[pltpu.VMEM(s.shape, s.dtype) for s in smalls]
        + [pltpu.SemaphoreType.DMA((5,)), pltpu.SemaphoreType.DMA((5,))],
        compiler_params=pltpu.CompilerParams(
            vmem_limit_bytes=60 * 1024 * 1024,
            dimension_semantics=("arbitrary",),
        ),
        name="assemble",
    )(comm, *smalls)


def fused_on_device(
    grad_values, grad_scales, master, first_moment, first_scale, second_moment, second_scale
):
    def flat(array):
        return array.reshape(array.shape[-2:])

    comm, *smalls = exchange(
        flat(grad_values),
        flat(grad_scales).T,
        flat(master),
        flat(first_moment),
        flat(first_scale),
        flat(second_moment),
        flat(second_scale),
    )
    weights, transposed, *smalls = assemble(comm, smalls)
    return tuple(array[None] for array in (*smalls, weights, transposed))


def expand(values, scales):
    shape = values.shape
    blocks = values.astype(f32).reshape(shape[:-1] + (shape[-1] // BLOCK, BLOCK))
    return (blocks * scales.astype(f32)[..., None]).reshape(shape)


def quantize_blocks(values, signed):
    shape = values.shape
    blocks = values.reshape(shape[:-1] + (shape[-1] // BLOCK, BLOCK))
    if signed:
        peak = jnp.max(jnp.abs(blocks), axis=-1) + scale_eps
    else:
        peak = jnp.max(blocks, axis=-1) + scale_eps
    coded = (blocks / peak[..., None]).astype(bf16).reshape(shape)
    return (coded, peak)


def adam_step(gradient, master, first_moment, first_scale, second_moment, second_scale):
    first = beta_one * expand(first_moment, first_scale) + (1.0 - beta_one) * gradient
    second = beta_two * expand(second_moment, second_scale) + (1.0 - beta_two) * gradient * gradient
    direction = first / corr_one / (jnp.sqrt(second / corr_two) + adam_eps)
    updated = master - rate * direction
    first_coded, first_peak = quantize_blocks(first, True)
    second_coded, second_peak = quantize_blocks(second, False)
    return (updated, first_coded, first_peak, second_coded, second_peak, updated.astype(bf16))


def on_device(
    grad_values, grad_scales, master, first_moment, first_scale, second_moment, second_scale
):
    arrived, arrived_scales = (
        lax.all_to_all(grad_values, "group", split_axis=3, concat_axis=1, tiled=True),
        lax.all_to_all(grad_scales, "group", split_axis=3, concat_axis=1, tiled=True),
    )
    partial_sum = jnp.sum(expand(arrived, arrived_scales), axis=1)
    partial_sum = partial_sum.reshape(master.shape)
    gradient = lax.psum(partial_sum, "node")
    result = adam_step(gradient, master, first_moment, first_scale, second_moment, second_scale)
    updated, first_coded, first_peak, second_coded, second_peak, low_weights = result
    weights = lax.all_gather(low_weights, "group", axis=1, tiled=True)
    transposed = jnp.swapaxes(weights, 1, 2)
    return (updated, first_coded, first_peak, second_coded, second_peak, weights, transposed)


def solution(mesh):
    placed = (
        P("node", "group", "fsdp", None, None),
        P("node", "group", "fsdp", None, None),
        P("fsdp", "group", None),
        P("fsdp", "group", None),
        P("fsdp", "group", None),
        P("fsdp", "group", None),
        P("fsdp", "group", None),
    )
    fused = mesh.shape["node"] == 1 and mesh.shape["group"] == 32
    return jax.shard_map(
        fused_on_device if fused else on_device,
        mesh=mesh,
        in_specs=placed,
        out_specs=(
            P("fsdp", "group", None),
            P("fsdp", "group", None),
            P("fsdp", "group", None),
            P("fsdp", "group", None),
            P("fsdp", "group", None),
            P("fsdp", None, None),
            P("fsdp", None, None),
        ),
        check_vma=False,
    )
```

```python
import functools

import jax
import jax.numpy as jnp
from jax import lax
from jax.experimental import pallas as pl
from jax.experimental.pallas import tpu as pltpu
from jax.sharding import PartitionSpec as P

BLOCK = 128
CHUNKS = 8
PARTS = (0, 3, 6, 8)
GROUPS = len(PARTS) - 1
TILE = 16

beta_one = 0.9
beta_two = 0.95
rate = 0.02
adam_eps = 1e-08
scale_eps = 1e-06
corr_one = 1.0 - 0.9**10
corr_two = 1.0 - 0.95**10

f32 = jnp.float32
bf16 = jnp.bfloat16


def exchange_kernel(
    grad, gscale, master_in, fm_in, fs_in, sm_in, ss_in,
    comm, master_out, first_out, fs_out, second_out, ss_out,
    own, sib, sc_own, sc_sib, sh_own, sh_sib, part, rx1, rx2, acc, rx3, gfull, fbase, sbase, slotf, slot, held,
    master, fm, fs, sm, ss, new_master, new_first, new_fs, new_second, new_ss,
    in_sem, out_sem, own_sem, sc_sem, sib_sem, p1_sem, p2_sem, z_sem, g_sem,
    az_sem, ax_sem, ay_sem, fx_sem, fy_sem, as_sem, loc_sem,
):
    w = grad.shape[1] // 2 // CHUNKS
    nb = w // BLOCK
    me = lax.axis_index("group")
    c = lax.rem(me, 2)
    x = lax.rem(me // 2, 2)
    y = lax.rem(me // 4, 2)
    z = me // 8

    def index(zz, yy, xx, cc):
        return zz * 8 + yy * 4 + xx * 2 + cc

    sibling = index(z, y, x, 1 - c)
    xn = index(z, y, 1 - x, c)
    yn = index(z, 1 - y, x, c)
    z_up = [lax.rem(z + d, 4) for d in range(4)]
    z_from = [lax.rem(z + 4 - d, 4) for d in range(4)]
    zn = [index(z_up[d], y, x, c) for d in range(4)]

    def remote(src, dst, sems, at, to):
        return pltpu.make_async_remote_copy(
            src_ref=src,
            dst_ref=dst,
            send_sem=sems.at[(0,) + at],
            recv_sem=sems.at[(1,) + at],
            device_id={"group": to},
            device_id_type=pl.DeviceIdType.MESH,
        )

    sent = []

    def send(*args):
        copy = remote(*args)
        copy.start()
        sent.append(copy)
        return copy

    def local(src, dst, sem):
        copy = pltpu.make_async_copy(src, dst, sem)
        copy.start()
        return copy

    def columns(k, h):
        return k * 2 * w + h * w

    scale_own = local(gscale, sc_own, in_sem.at[5])
    own_copies = []
    for k in range(CHUNKS):
        here = pl.multiple_of(columns(k, c), BLOCK)
        own_copies.append(local(grad.at[:, pl.ds(here, w)], own.at[k], own_sem.at[k]))

    barrier = pltpu.get_barrier_semaphore()
    partners = [sibling, xn, yn] + zn[1:]
    for to in partners:
        pl.semaphore_signal(
            barrier, inc=1, device_id={"group": to}, device_id_type=pl.DeviceIdType.MESH
        )
    pl.semaphore_wait(barrier, len(partners))

    scale_copy = send(gscale, sc_sib, sc_sem, (0,), sibling)
    sib_copies = []
    for k in range(CHUNKS):
        there = pl.multiple_of(columns(k, 1 - c), BLOCK)
        sib_copies.append(send(grad.at[:, pl.ds(there, w)], sib.at[k], sib_sem, (k,), sibling))
    fetched = [
        local(src, dst, in_sem.at[i])
        for i, (src, dst) in enumerate(
            ((fm_in, fm), (fs_in, fs), (sm_in, sm), (ss_in, ss), (master_in, master))
        )
    ]

    def half_scales(ref, out):
        values = ref[...].astype(f32).T
        for k in range(CHUNKS):
            j = 2 * k * nb
            out[:, k * nb : (k + 1) * nb] = jnp.where(
                c == 0, values[:, j : j + nb], values[:, j + nb : j + 2 * nb]
            )

    scale_own.wait()
    half_scales(sc_own, sh_own)
    scale_copy.wait_recv()
    half_scales(sc_sib, sh_sib)

    def order(k):
        return (x, y, xn, yn) if k % 2 == 0 else (y, x, yn, xn)

    p1, p2 = {}, {}

    def core_sum(k):
        own_copies[k].wait()
        sib_copies[k].wait_recv()

        def body(i, carry):
            rows = pl.ds(pl.multiple_of(i * 16, 16), 16)
            so, sb = sh_own[rows, :], sh_sib[rows, :]
            zz, yy = i // 2, lax.rem(i, 2)
            for b in range(nb):
                j = k * nb + b
                cols = pl.ds(b * BLOCK, BLOCK)
                v = own[k, rows, cols].astype(f32) * so[:, j : j + 1]
                v += sib[k, rows, cols].astype(f32) * sb[:, j : j + 1]
                for xx in range(2):
                    one, two = (xx, yy) if k % 2 == 0 else (yy, xx)
                    part[k, one, two, zz, :, cols] = v[8 * xx : 8 * xx + 8]
            return carry

        lax.fori_loop(0, 8, body, 0)
        a, _, an, _ = order(k)
        p1[k] = send(part.at[k, 1 - a], rx1.at[k], p1_sem, (k,), an)

    def base(k):
        for b in range(2 * nb):
            j = 2 * k * nb + b
            cols = pl.ds(j * BLOCK, BLOCK)
            fbase[:, cols] = beta_one * (fm[:, cols].astype(f32) * fs[:, j : j + 1])
            sbase[:, cols] = beta_two * (sm[:, cols].astype(f32) * ss[:, j : j + 1])

    def first_axis(k):
        a, b, _, bn = order(k)
        p1[k].wait_recv()
        for zz in range(4):
            part[k, a, 1 - b, zz] = part[k, a, 1 - b, zz] + rx1[k, 1 - b, zz]
        p2[k] = send(part.at[k, a, 1 - b], rx2.at[k], p2_sem, (k,), bn)

    def second_axis(k):
        a, b, _, _ = order(k)
        p2[k].wait_recv()
        for zz in range(4):
            acc[k, zz] = part[k, a, b, zz] + rx1[k, b, zz] + rx2[k, zz]
        for d in range(1, 4):
            send(acc.at[k, z_up[d]], rx3.at[k, d], z_sem, (k, d), zn[d])

    def along_z(k):
        total = acc[k, z]
        for d in range(1, 4):
            remote(acc.at[k, z_up[d]], rx3.at[k, d], z_sem, (k, d), zn[d]).wait_recv()
            total = total + rx3[k, d]
        gfull[c, k] = total
        send(gfull.at[c, k], gfull.at[c, k], g_sem, (k,), sibling)

    def adam(k):
        remote(gfull.at[1 - c, k], gfull.at[1 - c, k], g_sem, (k,), sibling).wait_recv()
        for h in range(2):
            cols = pl.ds(columns(k, h), w)
            v = gfull[h, k]
            g = jnp.where(c == 0, v[0:4], v[4:8])
            first = fbase[:, cols] + (1.0 - beta_one) * g
            second = sbase[:, cols] + (1.0 - beta_two) * g * g
            fbase[:, cols] = first
            sbase[:, cols] = second
            direction = first / corr_one / (jnp.sqrt(second / corr_two) + adam_eps)
            updated = master[:, cols] - rate * direction
            new_master[:, cols] = updated
            for q in range(2):
                r = 4 * (2 * h + q)
                slotf[r : r + 4, k * (w // 2) : (k + 1) * (w // 2)] = updated[
                    :, q * (w // 2) : (q + 1) * (w // 2)
                ]

    def quantize(k):
        for b in range(2 * nb):
            j = 2 * k * nb + b
            cols = pl.ds(j * BLOCK, BLOCK)
            first, second = fbase[:, cols], sbase[:, cols]
            peak = jnp.max(jnp.abs(first), axis=1, keepdims=True) + scale_eps
            new_fs[:, j : j + 1] = peak
            new_first[:, cols] = (first / peak).astype(bf16)
            peak = jnp.max(second, axis=1, keepdims=True) + scale_eps
            new_ss[:, j : j + 1] = peak
            new_second[:, cols] = (second / peak).astype(bf16)

    wide = w // 2
    placed = []

    def place(e, yy, xx, cc, first=0, count=4):
        row = pl.multiple_of((index(0, yy, xx, cc) * 4 + first) * TILE, TILE)
        return held.at[PARTS[e] : PARTS[e + 1], pl.ds(row, count * TILE)]

    def gather_own(e):
        for k in chunks(e):
            slot[k] = slotf[:, k * wide : (k + 1) * wide].astype(bf16)
        src, dst = slot.at[PARTS[e] : PARTS[e + 1]], place(e, y, x, c, z, 1)
        for d in range(1, 4):
            send(src, dst, az_sem, (e, d), zn[d])
        placed.append(local(src, dst, loc_sem.at[e]))

    def gather_z(e):
        placed[e].wait()
        for d in range(1, 4):
            ref = place(e, y, x, c, z_from[d], 1)
            remote(ref, ref, az_sem, (e, d), zn[d]).wait_recv()
        ref = place(e, y, x, c)
        send(ref, ref, ax_sem, (e,), xn)
        send(ref, ref, ay_sem, (e,), yn)
        send(ref, ref, as_sem, (e, 0), sibling)

    def gather_xy(e):
        ref = place(e, y, 1 - x, c)
        remote(ref, ref, ax_sem, (e,), xn).wait_recv()
        right = place(e, y, 1 - x, c, 2, 2)
        send(right, right, fy_sem, (e,), yn)
        other = place(e, 1 - y, x, c)
        remote(other, other, ay_sem, (e,), yn).wait_recv()
        left = place(e, 1 - y, x, c, 0, 2)
        send(left, left, fx_sem, (e,), xn)
        send(ref, ref, as_sem, (e, 1), sibling)
        send(other, other, as_sem, (e, 2), sibling)

    def gather_far(e):
        left = place(e, 1 - y, 1 - x, c, 0, 2)
        right = place(e, 1 - y, 1 - x, c, 2, 2)
        remote(left, left, fx_sem, (e,), xn).wait_recv()
        remote(right, right, fy_sem, (e,), yn).wait_recv()
        ref = place(e, 1 - y, 1 - x, c)
        send(ref, ref, as_sem, (e, 3), sibling)

    def gather_end(e):
        for q in range(4):
            yy = 1 - y if q >= 2 else y
            xx = 1 - x if q % 2 == 1 else x
            ref = place(e, yy, xx, 1 - c)
            remote(ref, ref, as_sem, (e, q), sibling).wait_recv()
        part_of = slice(PARTS[e], PARTS[e + 1])
        return local(held.at[part_of], comm.at[part_of], loc_sem.at[e])

    def chunks(e):
        return range(PARTS[e], PARTS[e + 1])

    def each(f, e):
        if 0 <= e < GROUPS:
            for k in chunks(e):
                f(k)

    def group(f, e):
        if 0 <= e < GROUPS:
            f(e)

    ahead = 2
    for e in range(ahead):
        each(core_sum, e)
    for copy in fetched:
        copy.wait()
    for e in range(ahead):
        each(base, e)
    for t in range(GROUPS + 5):
        each(first_axis, t)
        each(core_sum, t + ahead)
        each(base, t + ahead)
        each(second_axis, t - 1)
        each(along_z, t - 2)
        each(adam, t - 2)
        group(gather_own, t - 2)
        group(gather_z, t - 3)
        group(gather_xy, t - 4)
        group(gather_far, t - 5)
        each(quantize, t - 3)
    stored = [
        local(src, dst, out_sem.at[i])
        for i, (src, dst) in enumerate(
            (
                (new_master, master_out),
                (new_first, first_out),
                (new_fs, fs_out),
                (new_second, second_out),
                (new_ss, ss_out),
            )
        )
    ]
    for e in range(GROUPS):
        stored.append(gather_end(e))
    for copy in sent:
        copy.wait_send()
    for copy in stored:
        copy.wait()


def exchange(grad, gscale, master, fm, fs, sm, ss):
    rows, d = grad.shape
    own_rows = master.shape[0]
    w = d // 2 // CHUNKS
    K, G = CHUNKS, GROUPS
    anywhere = pl.BlockSpec(memory_space=pl.ANY)
    dma = pltpu.SemaphoreType.DMA
    smalls = (master, fm, fs, sm, ss)
    return pl.pallas_call(
        exchange_kernel,
        out_shape=(jax.ShapeDtypeStruct((K, rows * 4, d // 4 // K), bf16),)
        + tuple(jax.ShapeDtypeStruct(s.shape, s.dtype) for s in smalls),
        in_specs=[anywhere] * 7,
        out_specs=(anywhere,) * 6,
        scratch_shapes=[
            pltpu.VMEM((K, rows, w), bf16),
            pltpu.VMEM((K, rows, w), bf16),
            pltpu.VMEM(gscale.shape, bf16),
            pltpu.VMEM(gscale.shape, bf16),
            pltpu.VMEM((rows, gscale.shape[0] // 2), f32),
            pltpu.VMEM((rows, gscale.shape[0] // 2), f32),
            pltpu.VMEM((K, 2, 2, 4, 8, w), f32),
            pltpu.VMEM((K, 2, 4, 8, w), f32),
            pltpu.VMEM((K, 4, 8, w), f32),
            pltpu.VMEM((K, 4, 8, w), f32),
            pltpu.VMEM((K, 4, 8, w), f32),
            pltpu.VMEM((2, K, 8, w), f32),
            pltpu.VMEM((own_rows, d), f32),
            pltpu.VMEM((own_rows, d), f32),
            pltpu.VMEM((TILE, d // 4), f32),
            pltpu.VMEM((K, TILE, d // 4 // K), bf16),
            pltpu.VMEM((K, rows * 4, d // 4 // K), bf16),
        ]
        + [pltpu.VMEM(s.shape, s.dtype) for s in smalls + smalls]
        + [
            dma((6,)),
            dma((5,)),
            dma((K,)),
            dma((2, 1)),
            dma((2, K)),
            dma((2, K)),
            dma((2, K)),
            dma((2, K, 4)),
            dma((2, K)),
            dma((2, G, 4)),
            dma((2, G)),
            dma((2, G)),
            dma((2, G)),
            dma((2, G)),
            dma((2, G, 4)),
            dma((G,)),
        ],
        compiler_params=pltpu.CompilerParams(
            collective_id=0, has_side_effects=True, vmem_limit_bytes=60 * 1024 * 1024
        ),
        cost_estimate=pl.CostEstimate(
            flops=8 * rows * d, bytes_accessed=8 * rows * d, transcendentals=own_rows * d
        ),
        name="exchange",
    )(grad, gscale, master, fm, fs, sm, ss)


def assemble_kernel(comm, *refs):
    smalls, (weights, transposed), copied = refs[:5], refs[5:7], refs[7:12]
    staged, in_sem, out_sem = refs[12:17], refs[17], refs[18]
    t = pl.program_id(0)
    cols = comm.shape[2]
    step = 2 * BLOCK
    loads = [pltpu.make_async_copy(a, b, in_sem.at[i]) for i, (a, b) in enumerate(zip(smalls, staged))]
    stores = [pltpu.make_async_copy(a, b, out_sem.at[i]) for i, (a, b) in enumerate(zip(staged, copied))]

    @pl.when(t == 0)
    def _():
        for copy in loads:
            copy.start()

    @pl.when(t == 2)
    def _():
        for copy in loads:
            copy.wait()
        for copy in stores:
            copy.start()

    for z in range(4):
        for u in range(2):
            slots = [4 * (4 * u + i) + z for i in range(4)]
            found = [comm[0, TILE * n : TILE * (n + 1), :].astype(f32) for n in slots]
            row = 32 * z + 16 * u
            for kk in range(4):
                rows = jnp.concatenate([v[4 * kk : 4 * kk + 4] for v in found], axis=0)
                weights[row : row + 16, kk * cols : (kk + 1) * cols] = rows.astype(bf16)
    for i in range(4 * cols // step):
        block = weights[:, i * step : (i + 1) * step]
        transposed[i * step : (i + 1) * step, :] = block.T

    @pl.when(t == pl.num_programs(0) - 1)
    def _():
        for copy in stores:
            copy.wait()


def assemble(comm, smalls):
    rows = comm.shape[1] // 4
    d = comm.shape[0] * comm.shape[2] * 4
    cols = d // 4 // CHUNKS
    anywhere = pl.BlockSpec(memory_space=pl.ANY)
    return pl.pallas_call(
        assemble_kernel,
        grid=(CHUNKS,),
        out_shape=(
            jax.ShapeDtypeStruct((rows, d), bf16),
            jax.ShapeDtypeStruct((d, rows), bf16),
        )
        + tuple(jax.ShapeDtypeStruct(s.shape, s.dtype) for s in smalls),
        in_specs=[pl.BlockSpec((1, rows * 4, cols), lambda k: (k, 0, 0))]
        + [anywhere] * 5,
        out_specs=(
            pl.BlockSpec((rows, 4 * cols), lambda k: (0, k)),
            pl.BlockSpec((4 * cols, rows), lambda k: (k, 0)),
        )
        + (anywhere,) * 5,
        scratch_shapes=[pltpu.VMEM(s.shape, s.dtype) for s in smalls]
        + [pltpu.SemaphoreType.DMA((5,)), pltpu.SemaphoreType.DMA((5,))],
        compiler_params=pltpu.CompilerParams(
            vmem_limit_bytes=60 * 1024 * 1024,
            dimension_semantics=("arbitrary",),
        ),
        name="assemble",
    )(comm, *smalls)


def fused_on_device(
    grad_values, grad_scales, master, first_moment, first_scale, second_moment, second_scale
):
    def flat(array):
        return array.reshape(array.shape[-2:])

    comm, *smalls = exchange(
        flat(grad_values),
        flat(grad_scales).T,
        flat(master),
        flat(first_moment),
        flat(first_scale),
        flat(second_moment),
        flat(second_scale),
    )
    weights, transposed, *smalls = assemble(comm, smalls)
    return tuple(array[None] for array in (*smalls, weights, transposed))


def expand(values, scales):
    shape = values.shape
    blocks = values.astype(f32).reshape(shape[:-1] + (shape[-1] // BLOCK, BLOCK))
    return (blocks * scales.astype(f32)[..., None]).reshape(shape)


def quantize_blocks(values, signed):
    shape = values.shape
    blocks = values.reshape(shape[:-1] + (shape[-1] // BLOCK, BLOCK))
    if signed:
        peak = jnp.max(jnp.abs(blocks), axis=-1) + scale_eps
    else:
        peak = jnp.max(blocks, axis=-1) + scale_eps
    coded = (blocks / peak[..., None]).astype(bf16).reshape(shape)
    return (coded, peak)


def adam_step(gradient, master, first_moment, first_scale, second_moment, second_scale):
    first = beta_one * expand(first_moment, first_scale) + (1.0 - beta_one) * gradient
    second = beta_two * expand(second_moment, second_scale) + (1.0 - beta_two) * gradient * gradient
    direction = first / corr_one / (jnp.sqrt(second / corr_two) + adam_eps)
    updated = master - rate * direction
    first_coded, first_peak = quantize_blocks(first, True)
    second_coded, second_peak = quantize_blocks(second, False)
    return (updated, first_coded, first_peak, second_coded, second_peak, updated.astype(bf16))


def on_device(
    grad_values, grad_scales, master, first_moment, first_scale, second_moment, second_scale
):
    arrived, arrived_scales = (
        lax.all_to_all(grad_values, "group", split_axis=3, concat_axis=1, tiled=True),
        lax.all_to_all(grad_scales, "group", split_axis=3, concat_axis=1, tiled=True),
    )
    partial_sum = jnp.sum(expand(arrived, arrived_scales), axis=1)
    partial_sum = partial_sum.reshape(master.shape)
    gradient = lax.psum(partial_sum, "node")
    result = adam_step(gradient, master, first_moment, first_scale, second_moment, second_scale)
    updated, first_coded, first_peak, second_coded, second_peak, low_weights = result
    weights = lax.all_gather(low_weights, "group", axis=1, tiled=True)
    transposed = jnp.swapaxes(weights, 1, 2)
    return (updated, first_coded, first_peak, second_coded, second_peak, weights, transposed)


def solution(mesh):
    placed = (
        P("node", "group", "fsdp", None, None),
        P("node", "group", "fsdp", None, None),
        P("fsdp", "group", None),
        P("fsdp", "group", None),
        P("fsdp", "group", None),
        P("fsdp", "group", None),
        P("fsdp", "group", None),
    )
    fused = mesh.shape["node"] == 1 and mesh.shape["group"] == 32
    return jax.shard_map(
        fused_on_device if fused else on_device,
        mesh=mesh,
        in_specs=placed,
        out_specs=(
            P("fsdp", "group", None),
            P("fsdp", "group", None),
            P("fsdp", "group", None),
            P("fsdp", "group", None),
            P("fsdp", "group", None),
            P("fsdp", None, None),
            P("fsdp", None, None),
        ),
        check_vma=False,
    )
```
